1024 devices in a mesh: wave: 64 (over x, z), lev: 16 (over y, core).
Axes of the slice: x: 8, y: 8, z: 8, core: 2. Of those that a mesh axis runs over, the one named last changes fastest.
Arguments:
- spectrum: bfloat16 [1024, 1024, 96, 6], P('wave', None, 'lev'), may hold values from -0.3125 to 0.3125
- legendre: bfloat16 [1024, 1024, 128], P('wave'), may hold values from -0.1875 to 0.1875
- wave_numbers: int32 [1024], replicated, may hold values from 0 to 1023, as said below
- vertical: float32 [96, 96], replicated, may hold values from -0.625 to 0.625
Outputs:
- tracer: float32 [96, 256, 2048], P(None, 'wave', 'lev')
The draws below stay inside these ranges and needn't reach their ends.
Inputs may be any that keep to these rules, and one draw needn't show every extreme that they name: wave_numbers is a permutation of 0 to 1023 in which slots 2 i and 2 i + 1 hold m and 1023 - m for some m, in either order.
All inputs are finite; a program needn't handle non-finite values.
Results may differ from the reference program's by a relative error of at most 0.0066.
Values may be sent and summed in bfloat16 or wider, within the bound.
A program may use at most 64 MiB of HBM per device.

```python
import math
import jax
import jax.numpy as jnp
from jax import lax

NM = 1024
LEV = 96
NLAT = 256
NLON = 2048


def draw_wave_numbers(key, part):
    order = jax.random.permutation(jax.random.fold_in(key, 11), NM // 2).astype(jnp.int32)
    flipped = jax.random.randint(jax.random.fold_in(key, 23), (NM // 2,), 0, 2).astype(jnp.int32)
    partner = (NM - 1 - order).astype(jnp.int32)
    leading = jnp.where(flipped == 1, partner, order)
    trailing = jnp.where(flipped == 1, order, partner)
    return jnp.stack([leading, trailing], axis=1).reshape(NM).astype(jnp.int32)


def block_levels(rng, extent, pieces, low, top_value):
    gain, own = 1.0, jax.random.fold_in(rng, 6)
    for position, shards_of in pieces:
        draws = jnp.exp(jax.random.uniform(jax.random.fold_in(own, position), (shards_of,), jnp.float32, low / len(pieces), top_value / len(pieces)))
        gain = gain * jnp.repeat(draws, extent[position] // shards_of).reshape([-1 if axis == position else 1 for axis in range(len(extent))])
    return gain


def gaussian(key, dims, deviation, bound, cuts=(), kind=jnp.bfloat16):
    values = jax.random.normal(key, dims, jnp.float32) * deviation
    if len(cuts) > 0:
        values = block_levels(key, dims, cuts, -0.22, 0.18) * values
    return jnp.clip(values, min=-bound, max=bound).astype(kind)


def setup_inputs(seed: int = 0) -> dict:
    seeds = jax.random.split(jax.random.key(seed), 5)
    return {
        "spectrum": gaussian(seeds[0], (NM, NM, LEV, 6), (0.7 / NM ** 0.5), 0.3125, ((0, 64), (2, 16))),
        "legendre": gaussian(seeds[1], (NM, NM, NLAT // 2), NM ** -0.5, 0.1875, ((0, 64),)),
        "wave_numbers": draw_wave_numbers(jax.random.fold_in(seeds[4], 71), 0),
        "vertical": gaussian(seeds[3], (LEV, LEV), LEV ** -0.5, 0.625, (), jnp.float32),
    }


courant_max = 0.45


def triangle_sums(spectrum_block, legendre_block, numbers):
    degree_count = spectrum_block.shape[1]
    degree = jnp.arange(degree_count, dtype=jnp.int32)
    counted = degree[None, :] < (degree_count - numbers)[:, None]
    even_mask = counted & (degree[None, :] % 2 == 0)
    odd_mask = counted & (degree[None, :] % 2 == 1)
    coefficient = spectrum_block.reshape(spectrum_block.shape[0], degree_count, -1).astype(jnp.float32)
    basis = legendre_block.astype(jnp.float32)
    zero_value = jnp.zeros((), jnp.float32)
    even_sums = jnp.einsum('skc,ski->sci', jnp.where(even_mask[:, :, None], coefficient, zero_value), basis)
    odd_sums = jnp.einsum('skc,ski->sci', jnp.where(odd_mask[:, :, None], coefficient, zero_value), basis)
    northern = even_sums + odd_sums
    southern = jnp.flip(even_sums - odd_sums, axis=2)
    return jnp.concatenate([northern, southern], axis=2).astype(jnp.bfloat16)


def twiddles(numbers):
    longitude = jnp.arange(NLON, dtype=jnp.int32)
    residue = (numbers[:, None] * longitude[None, :]) % NLON
    angles = residue.astype(jnp.float32) * (2.0 * math.pi / NLON)
    weight = jnp.where(numbers == 0, 1.0, 2.0).astype(jnp.float32)[:, None]
    return jnp.stack([weight * jnp.cos(angles), -weight * jnp.sin(angles)]).astype(jnp.bfloat16)


def upwind_core(extended, courant_x, courant_y):
    center = extended[:, 1:-1, 1:-1]
    western = extended[:, 1:-1, :-2]
    eastern = extended[:, 1:-1, 2:]
    northern = extended[:, :-2, 1:-1]
    southern = extended[:, 2:, 1:-1]
    return (center - jnp.maximum(courant_x, 0.0) * (center - western)
            - jnp.minimum(courant_x, 0.0) * (eastern - center)
            - jnp.maximum(courant_y, 0.0) * (center - northern)
            - jnp.minimum(courant_y, 0.0) * (southern - center))


def extend(field):
    padded = jnp.pad(field, ((0, 0), (1, 1), (0, 0)))
    return jnp.concatenate([padded[:, :, -1:], padded, padded[:, :, :1]], axis=2)


def reference(spectrum, legendre, wave_numbers, vertical):
    group = 16
    spectrum_blocks = spectrum.reshape(NM // group, group, NM, LEV * 6)
    legendre_blocks = legendre.reshape(NM // group, group, NM, NLAT // 2)
    number_blocks = wave_numbers.reshape(NM // group, group)
    fourier = lax.map(lambda packed: triangle_sums(packed[0], packed[1], packed[2]),
                      (spectrum_blocks, legendre_blocks, number_blocks))
    mode_groups = LEV // 16
    fourier = fourier.reshape(NM, mode_groups, 16, 3, 2, NLAT)
    fourier = jnp.moveaxis(fourier, 1, 0)
    twiddle = twiddles(wave_numbers).astype(jnp.float32)
    vertical_groups = jnp.moveaxis(vertical.reshape(LEV, mode_groups, 16), 1, 0)

    def accumulate(carry, packed):
        block, vertical_part = packed
        grid_values = jnp.einsum('smfrl,rsj->lmfj', block.astype(jnp.float32), twiddle)
        grid_values = grid_values.astype(jnp.bfloat16)
        term = jnp.einsum('vm,lmfj->fvlj', vertical_part, grid_values.astype(jnp.float32),
                          precision=lax.Precision.HIGHEST)
        return carry + term, None

    fields, _ = lax.scan(accumulate, jnp.zeros((3, LEV, NLAT, NLON), jnp.float32),
                         (fourier, vertical_groups))
    courant_x = courant_max * jnp.tanh(fields[0])
    courant_y = courant_max * jnp.tanh(fields[1])
    tracer = fields[2]
    for sweep in range(2):
        tracer = upwind_core(extend(tracer), courant_x, courant_y)
    return tracer
```

```python
import jax
import jax.numpy as jnp
import numpy as np
from jax import lax
from jax.experimental import pallas as pl
from jax.experimental.pallas import tpu as pltpu
from jax.sharding import PartitionSpec as P

BF = jnp.bfloat16
F32 = jnp.float32
MESH = pl.DeviceIdType.MESH
COURANT = 0.45

NM = 1024
NLON = 2048
LEVS = 96
WAVES = 64
LEVDEV = 16
SLOTS = 16
COLS = 36
MODES = 6
RADIX = 8
SPAN = NLON // RADIX

GROUPS = (
    ((0, 1), (1, 1), (0, 2), (1, 2)),
    ((0, 0), (1, 0), (2, 0), (2, 1)),
    ((2, 2), (2, 3), (1, 3), (0, 3)),
)
PLACE = {pair: (g, i) for g, group in enumerate(GROUPS) for i, pair in enumerate(group)}
EDGE_TILE = 6
OFFSETS = (-2, -1, 0, 127, 128, 129)


def fourier_table():
    numbers = np.arange(NM).reshape(NM // RADIX, RADIX).T
    residue = numbers[:, :, None] * np.arange(SPAN)[None, None, :] % NLON
    angle = residue * (2.0 * np.pi / NLON)
    weight = np.where(numbers == 0, 1.0, 2.0)[:, :, None]
    real, imaginary = weight * np.cos(angle), weight * np.sin(angle)
    imaginary = np.where(residue == 0, 0.0, imaginary)
    top = np.concatenate([real, imaginary], axis=2)
    bottom = np.concatenate([-imaginary, real], axis=2)
    return np.concatenate([top, bottom], axis=1).astype(BF)


def row_table():
    table = np.zeros((144, 256), np.float32)
    for (field, lat), (group, place) in PLACE.items():
        for mode in range(MODES):
            for part in range(2):
                pair = mode * 3 + field
                if pair < 16:
                    column = part * 64 + lat * 16 + pair
                else:
                    column = 128 + lat * 4 + (pair - 16) * 2 + part
                table[part * 72 + group * 24 + mode * 4 + place, column] = 1.0
    return table.astype(BF)


def edge_table():
    table = np.zeros((NLON, 128), np.float32)
    for block in range(LEVDEV):
        for k, offset in enumerate(OFFSETS):
            table[(block * 128 + offset) % NLON, block * 8 + k] = 1.0
    return table.astype(BF)


def spread_table():
    table = np.zeros((LEVS, 128), np.float32)
    for mode in range(LEVS):
        table[mode, mode // MODES * 8 + mode % MODES] = 1.0
    return table.astype(BF)


def dot(a, b):
    return jnp.dot(a, b, preferred_element_type=F32)


def pick(values, index):
    result = values[-1]
    for i in range(len(values) - 2, -1, -1):
        result = jnp.where(index == i, values[i], result)
    return result


def legendre_stage(numbers, spec, leg, copies, main, rest, wide, turned, tall, gather):
    for c in range(COLS + 4):
        values = spec[c if c < COLS else c - 4].astype(F32)
        for k in range(8):
            wide[k, c * SLOTS : (c + 1) * SLOTS, :] = values[:, k * 128 : (k + 1) * 128]
    degree = lax.broadcasted_iota(jnp.int32, (40, NM), 1)
    odd = degree % 2 == 1
    lane = lax.broadcasted_iota(jnp.int32, (32, 128), 1)
    turn = lane // 16 % 4
    small = lane // 4 % 4
    for s in range(SLOTS):
        if s % 4 == 0:
            copies[s // 4].wait()
        rows = jnp.concatenate(
            [
                jnp.concatenate(
                    [
                        wide[k, pl.ds(s, 16, stride=32), :],
                        wide[k, pl.ds(16 + s, 16, stride=32), :],
                        wide[k, pl.ds(512 + s, 8, stride=16), :],
                    ],
                    axis=0,
                )
                for k in range(8)
            ],
            axis=1,
        )
        rows = jnp.where(degree < NM - numbers(s), rows, 0.0)
        both = jnp.concatenate([rows, jnp.where(odd, -rows, rows)], axis=0).astype(BF)
        sums = dot(both, leg[s])
        for half in range(2):
            own = sums[half * 40 : (half + 1) * 40]
            block = jnp.concatenate([own[0:16]] * 4 + [own[16:32]] * 4, axis=0)
            turned[half, s % 2] = block.T
            lines = [turned[half, s % 2, pl.ds(r, 32, stride=4), :] for r in range(4)]
            if half == 1:
                lines = lines[::-1]
            gather[pl.ds(half * 512 + s, 32, stride=SLOTS), :] = pick(lines, turn)
            tall[half, s * 16 : (s + 1) * 16, :] = jnp.concatenate([own[32:40]] * 2, axis=0)
    for half in range(2):
        for h in range(2):
            turned[half, h] = tall[half, h * 128 : (h + 1) * 128, :].T
            lines = [turned[half, h, pl.ds(r, 32, stride=4), :] for r in range(4)]
            if half == 1:
                lines = lines[::-1]
            rest[half * 32 : (half + 1) * 32, h, :] = pick(lines, small)
    for b in range(WAVES):
        main[b] = gather[b * SLOTS : (b + 1) * SLOTS, :].astype(BF)


def choose_rows(numbers, choice):
    line = lax.broadcasted_iota(jnp.int32, (32, NM), 0)

    def step(i, carry):
        wanted = i // 4 + RADIX * (i % 4 * 32 + line)
        hit = jnp.where(numbers == wanted, 1.0, 0.0).astype(BF)
        choice[pl.ds(pl.multiple_of(i * 32, 32), 32), :] = hit
        return carry

    lax.fori_loop(0, 32, step, 0)


def fourier_stage(main, rest, choice, order, table, edges, message, small, joined, part, grid, edge):
    joined[:, 0:128] = main[...].reshape(NM, 128)
    for h in range(2):
        values = rest[:, h, :]
        for g in range(8):
            rolled = values if g == 0 else pltpu.roll(values, 128 - 16 * g, 1)
            small[pl.ds(h * 8 + g, WAVES, stride=SLOTS), :] = rolled
    joined[:, 128:256] = small[...].astype(BF)
    ordered = dot(choice[...], joined[...]).astype(BF)
    lines = lax.dot_general(
        order[...], ordered, (((1,), (1,)), ((), ())), preferred_element_type=F32
    )
    for k in range(RADIX):
        own = lines[:, k * 128 : (k + 1) * 128]
        pair = jnp.concatenate([own[0:72].astype(BF), own[72:144].astype(BF)], axis=1)
        part[k] = dot(pair, table[k])
    root = 0.5**0.5

    def combine(i, carry):
        row = pl.ds(pl.multiple_of(i * 8, 8), 8)
        tile = i + jnp.where(i >= EDGE_TILE, 1, 0)
        for h in range(2):
            re = [part[k, row, h * 128 : (h + 1) * 128] for k in range(RADIX)]
            im = [
                None if k % 4 == 0 else part[k, row, SPAN + h * 128 : SPAN + (h + 1) * 128]
                for k in range(RADIX)
            ]
            plus, minus = re[0] + re[4], re[0] - re[4]
            level, cross = re[2] + re[6], im[6] - im[2]
            even = [plus + level, minus + cross, plus - level, minus - cross]
            a, b = re[1] - re[5], re[7] - re[3]
            c, d = im[5] - im[1], im[7] - im[3]
            odd = [
                re[1] + re[3] + re[5] + re[7],
                root * (a + b + c + d),
                im[3] - im[1] + im[7] - im[5],
                root * (c + d - a - b),
            ]
            for u in range(RADIX):
                value = even[u % 4] + odd[u] if u < 4 else even[u % 4] - odd[u - 4]
                message[2 * u + h, tile] = value.astype(BF)
                grid[row, u * SPAN + h * 128 : u * SPAN + (h + 1) * 128] = value
        return carry

    lax.fori_loop(0, 9, combine, 0)
    edge[0:72] = dot(grid[...].astype(BF), edges[...])
    edge[72:80] = jnp.zeros((8, 128), F32)
    lane = lax.broadcasted_iota(jnp.int32, (8, 128), 1) // 8

    def pack(block, carry):
        total = jnp.zeros((8, 128), F32)
        for field in range(3):
            for lat in range(4):
                group, place = PLACE[(field, lat)]
                q = field * 4 + lat
                values = edge[pl.ds(group * 24 + place, 8, stride=4), :]
                rolled = pltpu.roll(values, (128 + 8 * q - 8 * block) % 128, 1)
                total = jnp.where(lane == q, rolled, total)
        message[block, EDGE_TILE] = total.astype(BF)
        return carry

    lax.fori_loop(0, LEVDEV, pack, 0)


def vertical_stage(band, own, north, south, vertical, spread, out, wide, fields, edges):
    sources = ((own, 0), (own, 3), (own, 7), (north, 1), (south, 0))
    for i, (ref, tile) in enumerate(sources):
        for d in range(LEVDEV):
            values = ref[d, tile : tile + 3].astype(F32)
            wide[i, d * 24 : (d + 1) * 24, :] = values.reshape(24, 128)
    top = vertical[...].astype(BF)
    low = (vertical[...] - top.astype(F32)).astype(BF)
    both = jnp.concatenate([top, low], axis=0)
    for i in range(5):
        for q in range(0, 4, 2):
            modes = jnp.concatenate(
                [wide[i, pl.ds(q, LEVS, stride=4), :], wide[i, pl.ds(q + 1, LEVS, stride=4), :]],
                axis=1,
            ).astype(BF)
            twice = dot(both, modes)
            value = twice[:LEVS] + twice[LEVS:]
            fields[i, q] = value[:, :128]
            fields[i, q + 1] = value[:, 128:]
    both = dot(both, spread[...]).astype(BF)
    for i, (ref, tile) in enumerate(((own, EDGE_TILE), (north, 0), (south, 3))):
        values = ref[:, tile].reshape(128, 128)
        twice = dot(both, values)
        edges[i] = twice[:LEVS] + twice[LEVS:]

    lane = lax.broadcasted_iota(jnp.int32, (8, 128), 1)
    first, last = band == 0, band == WAVES - 1

    def where_is(field, lat):
        if lat < 0:
            group, place = PLACE[(field, lat + 4)]
            return 3, place
        if lat > 3:
            group, place = PLACE[(field, lat - 4)]
            return 4, place
        return PLACE[(field, lat)]

    def shift(value, amount):
        amount = amount % 128
        return value if amount == 0 else pltpu.roll(value, amount, 1)

    def upwind(center, west, east, north, south, cx, cy):
        return (
            center
            - jnp.maximum(cx, 0.0) * (center - west)
            - jnp.minimum(cx, 0.0) * (east - center)
            - jnp.maximum(cy, 0.0) * (center - north)
            - jnp.minimum(cy, 0.0) * (south - center)
        )

    def line(step, carry):
        level = pl.ds(pl.multiple_of(step * 8, 8), 8)

        def field(f, lat):
            i, q = where_is(f, lat)
            return fields[i, q, level, :]

        def courant(value):
            return COURANT * jnp.tanh(value)

        zero = jnp.zeros((8, 128), F32)
        tracer = {lat: field(2, lat) for lat in range(-2, 6)}
        for lat in (-2, -1):
            tracer[lat] = jnp.where(first, zero, tracer[lat])
        for lat in (4, 5):
            tracer[lat] = jnp.where(last, zero, tracer[lat])
        cx = {lat: courant(field(0, lat)) for lat in range(-1, 5)}
        cy = {lat: courant(field(1, lat)) for lat in range(-1, 5)}
        mine, upper, lower = edges[0, level, :], edges[1, level, :], edges[2, level, :]

        def side(f):
            return jnp.where(
                lane < 16,
                shift(upper, -(f * 32 + 16)),
                jnp.where(lane < 48, shift(mine, 16 - f * 32), shift(lower, 48 - f * 32)),
            )

        edge = side(2)
        edge = jnp.where(((lane < 16) & first) | ((lane >= 48) & last), zero, edge)
        edge_x, edge_y = courant(side(0)), courant(side(1))

        def beside(value, rim, lat):
            west = shift(value, 1)
            west = jnp.where(lane == 0, shift(rim, -((lat + 2) * 8 + 1)), west)
            east = shift(value, -1)
            east = jnp.where(lane == 127, shift(rim, 127 - ((lat + 2) * 8 + 4)), east)
            return west, east

        once = {}
        for lat in range(-1, 5):
            west, east = beside(tracer[lat], edge, lat)
            once[lat] = upwind(
                tracer[lat], west, east, tracer[lat - 1], tracer[lat + 1], cx[lat], cy[lat]
            )
        once[-1] = jnp.where(first, zero, once[-1])
        once[4] = jnp.where(last, zero, once[4])
        rim = upwind(
            edge, shift(edge, 1), shift(edge, -1), shift(edge, 8), shift(edge, -8), edge_x, edge_y
        )
        for lat in range(4):
            west, east = beside(once[lat], rim, lat)
            out[level, lat, :] = upwind(
                once[lat], west, east, once[lat - 1], once[lat + 1], cx[lat], cy[lat]
            )
        return carry

    lax.fori_loop(0, LEVS // 8, line, 0)


def kernel_a(numbers, spec, leg, main, rest, leg_here, sem, wide, turned, tall, gather):
    copies = []
    for i in range(4):
        copy = pltpu.make_async_copy(
            leg.at[4 * i : 4 * i + 4], leg_here.at[4 * i : 4 * i + 4], sem.at[i]
        )
        copy.start()
        copies.append(copy)
    first = lax.axis_index("wave") * SLOTS
    legendre_stage(
        lambda s: numbers[first + s], spec, leg_here, copies, main, rest, wide, turned, tall, gather
    )


def send_rows(w):
    return jnp.where(w < WAVES // 2, w, 95 - w)


def kernel_t1(main, rest, main_out, rest_out, send, recv, here):
    w = lax.axis_index("wave")
    barrier = pltpu.get_barrier_semaphore()

    def greet(i, carry):
        pl.semaphore_signal(
            barrier, inc=1, device_id={"wave": lax.rem(w + i, WAVES)}, device_id_type=MESH
        )
        return carry

    lax.fori_loop(1, WAVES, greet, 0)
    pl.semaphore_wait(barrier, WAVES - 1)

    def go(i, carry):
        target = lax.rem(w + i, WAVES)
        row = send_rows(target)
        for j, (src, dst) in enumerate(((main, main_out), (rest, rest_out))):
            pltpu.make_async_remote_copy(
                src_ref=src.at[row],
                dst_ref=dst.at[w],
                send_sem=send.at[j],
                recv_sem=recv.at[j],
                device_id={"wave": target},
                device_id_type=MESH,
            ).start()
        return carry

    lax.fori_loop(1, WAVES, go, 0)
    row = send_rows(w)
    local = [
        pltpu.make_async_copy(src.at[row], dst.at[w], here.at[j])
        for j, (src, dst) in enumerate(((main, main_out), (rest, rest_out)))
    ]
    for copy in local:
        copy.start()
    for copy in local:
        copy.wait()
    many = pl.ds(0, WAVES - 1)
    for j, (src, dst) in enumerate(((main, main_out), (rest, rest_out))):
        whole = pltpu.make_async_remote_copy(
            src_ref=src.at[many],
            dst_ref=dst.at[many],
            send_sem=send.at[j],
            recv_sem=recv.at[j],
            device_id={"wave": lax.rem(w + 1, WAVES)},
            device_id_type=MESH,
        )
        whole.wait_send()
        whole.wait_recv()


def kernel_b(main, rest, numbers, order, table, edges, message, choice, small, joined, part, grid, edge):
    choose_rows(numbers[...], choice)
    fourier_stage(
        main, rest, choice, order, table, edges, message, small, joined, part, grid, edge
    )


def kernel_t2(message, own, north, south, send, recv, here, halo_send, halo_recv):
    w, v = lax.axis_index("wave"), lax.axis_index("lev")
    barrier = pltpu.get_barrier_semaphore()

    def greet(i, carry):
        pl.semaphore_signal(
            barrier, inc=1, device_id={"lev": lax.rem(v + i, LEVDEV)}, device_id_type=MESH
        )
        return carry

    lax.fori_loop(1, LEVDEV, greet, 0)
    upper, lower = lax.rem(w + WAVES - 1, WAVES), lax.rem(w + 1, WAVES)
    for other in (upper, lower):
        pl.semaphore_signal(barrier, inc=1, device_id={"wave": other}, device_id_type=MESH)
    pl.semaphore_wait(barrier, LEVDEV + 1)

    def go(i, carry):
        target = lax.rem(v + i, LEVDEV)
        pltpu.make_async_remote_copy(
            src_ref=message.at[target],
            dst_ref=own.at[v],
            send_sem=send,
            recv_sem=recv,
            device_id={"lev": target},
            device_id_type=MESH,
        ).start()
        return carry

    lax.fori_loop(1, LEVDEV, go, 0)
    local = pltpu.make_async_copy(message.at[v], own.at[v], here)
    local.start()
    local.wait()
    many = pl.ds(0, LEVDEV - 1)
    whole = pltpu.make_async_remote_copy(
        src_ref=message.at[many],
        dst_ref=own.at[many],
        send_sem=send,
        recv_sem=recv,
        device_id={"lev": lax.rem(v + 1, LEVDEV)},
        device_id_type=MESH,
    )
    whole.wait_send()
    whole.wait_recv()
    down = pltpu.make_async_remote_copy(
        src_ref=own.at[:, 6:10],
        dst_ref=north,
        send_sem=halo_send.at[0],
        recv_sem=halo_recv.at[0],
        device_id={"wave": lower},
        device_id_type=MESH,
    )
    up = pltpu.make_async_remote_copy(
        src_ref=own.at[:, 3:7],
        dst_ref=south,
        send_sem=halo_send.at[1],
        recv_sem=halo_recv.at[1],
        device_id={"wave": upper},
        device_id_type=MESH,
    )
    down.start()
    up.start()
    down.wait()
    up.wait()


def kernel_c(own, north, south, vertical, spread, out, wide, fields, edges):
    band = lax.axis_index("wave")
    vertical_stage(band, own, north, south, vertical, spread, out, wide, fields, edges)


VM = pl.BlockSpec(memory_space=pltpu.VMEM)
ANY = pl.BlockSpec(memory_space=pl.ANY)
SM = pl.BlockSpec(memory_space=pltpu.SMEM)


def params(**kw):
    return pltpu.CompilerParams(vmem_limit_bytes=40 * 2**20, **kw)


def body(spectrum, legendre, wave_numbers, vertical):
    spec = jnp.transpose(spectrum, (2, 3, 0, 1)).reshape(COLS, SLOTS, NM)
    shape = jax.ShapeDtypeStruct
    dma = pltpu.SemaphoreType.DMA
    pair = (shape((WAVES, SLOTS, 128), BF), shape((WAVES, 2, 128), F32))
    main, rest = pl.pallas_call(
        kernel_a,
        name="legendre",
        out_shape=pair,
        in_specs=[SM, VM, ANY],
        out_specs=(VM, VM),
        scratch_shapes=[
            pltpu.VMEM((SLOTS, NM, 128), BF),
            dma((4,)),
            pltpu.VMEM((8, 640, 128), F32),
            pltpu.VMEM((2, 2, 128, 128), F32),
            pltpu.VMEM((2, 256, 128), F32),
            pltpu.VMEM((WAVES * SLOTS, 128), F32),
        ],
        compiler_params=params(),
    )(wave_numbers, spec, legendre)
    main, rest = pl.pallas_call(
        kernel_t1,
        name="bands",
        out_shape=pair,
        in_specs=[VM, VM],
        out_specs=(VM, VM),
        scratch_shapes=[dma((2,)), dma((2,)), dma((2,))],
        compiler_params=params(collective_id=0, has_side_effects=True),
    )(main, rest)
    message = pl.pallas_call(
        kernel_b,
        name="fourier",
        out_shape=shape((LEVDEV, 10, 8, 128), BF),
        in_specs=[VM] * 6,
        out_specs=VM,
        scratch_shapes=[
            pltpu.VMEM((NM, NM), BF),
            pltpu.VMEM((NM, 128), F32),
            pltpu.VMEM((NM, 256), BF),
            pltpu.VMEM((RADIX, 72, 2 * SPAN), F32),
            pltpu.VMEM((72, NLON), F32),
            pltpu.VMEM((80, 128), F32),
        ],
        compiler_params=params(),
    )(
        main,
        rest,
        wave_numbers.reshape(1, NM),
        jnp.asarray(row_table()),
        jnp.asarray(fourier_table()),
        jnp.asarray(edge_table()),
    )
    own, north, south = pl.pallas_call(
        kernel_t2,
        name="longitudes",
        out_shape=(
            shape((LEVDEV, 10, 8, 128), BF),
            shape((LEVDEV, 4, 8, 128), BF),
            shape((LEVDEV, 4, 8, 128), BF),
        ),
        in_specs=[VM],
        out_specs=(VM, VM, VM),
        scratch_shapes=[dma(()), dma(()), dma(()), dma((2,)), dma((2,))],
        compiler_params=params(collective_id=1, has_side_effects=True),
    )(message)
    return pl.pallas_call(
        kernel_c,
        name="upwind",
        out_shape=shape((LEVS, 4, 128), F32),
        in_specs=[VM] * 5,
        out_specs=VM,
        scratch_shapes=[
            pltpu.VMEM((5, LEVDEV * 24, 128), F32),
            pltpu.VMEM((5, 4, LEVS, 128), F32),
            pltpu.VMEM((3, LEVS, 128), F32),
        ],
        compiler_params=params(),
    )(own, north, south, vertical, jnp.asarray(spread_table()))


def solution(mesh):
    placed = (P("wave", None, "lev", None), P("wave", None, None), P(), P())
    return jax.shard_map(
        body, mesh=mesh, in_specs=placed, out_specs=P(None, "wave", "lev"), check_vma=False
    )
```

```python
import jax
import jax.numpy as jnp
import numpy as np
from jax import lax
from jax.experimental import pallas as pl
from jax.experimental.pallas import tpu as pltpu
from jax.sharding import PartitionSpec as P

BF = jnp.bfloat16
F32 = jnp.float32
MESH = pl.DeviceIdType.MESH
COURANT = 0.45

NM = 1024
NLON = 2048
LEVS = 96
WAVES = 64
LEVDEV = 16
SLOTS = 16
COLS = 36
MODES = 6
RADIX = 8
SPAN = NLON // RADIX

GROUPS = (
    ((0, 1), (1, 1), (0, 2), (1, 2)),
    ((0, 0), (1, 0), (2, 0), (2, 1)),
    ((2, 2), (2, 3), (1, 3), (0, 3)),
)
PLACE = {pair: (g, i) for g, group in enumerate(GROUPS) for i, pair in enumerate(group)}
EDGE_TILE = 6
OFFSETS = (-2, -1, 0, 127, 128, 129)


def fourier_table():
    numbers = np.arange(NM).reshape(NM // RADIX, RADIX).T
    residue = numbers[:, :, None] * np.arange(SPAN)[None, None, :] % NLON
    angle = residue * (2.0 * np.pi / NLON)
    weight = np.where(numbers == 0, 1.0, 2.0)[:, :, None]
    real, imaginary = weight * np.cos(angle), weight * np.sin(angle)
    imaginary = np.where(residue == 0, 0.0, imaginary)
    top = np.concatenate([real, imaginary], axis=2)
    bottom = np.concatenate([-imaginary, real], axis=2)
    return np.concatenate([top, bottom], axis=1).astype(BF)


def row_table():
    table = np.zeros((144, 256), np.float32)
    for (field, lat), (group, place) in PLACE.items():
        for mode in range(MODES):
            for part in range(2):
                pair = mode * 3 + field
                if pair < 16:
                    column = part * 64 + lat * 16 + pair
                else:
                    column = 128 + lat * 4 + (pair - 16) * 2 + part
                table[part * 72 + group * 24 + mode * 4 + place, column] = 1.0
    return table.astype(BF)


def edge_table():
    table = np.zeros((NLON, 128), np.float32)
    for block in range(LEVDEV):
        for k, offset in enumerate(OFFSETS):
            table[(block * 128 + offset) % NLON, block * 8 + k] = 1.0
    return table.astype(BF)


def spread_table():
    table = np.zeros((LEVS, 128), np.float32)
    for mode in range(LEVS):
        table[mode, mode // MODES * 8 + mode % MODES] = 1.0
    return table.astype(BF)


def dot(a, b):
    return jnp.dot(a, b, preferred_element_type=F32)


def pick(values, index):
    result = values[-1]
    for i in range(len(values) - 2, -1, -1):
        result = jnp.where(index == i, values[i], result)
    return result


def legendre_stage(numbers, spec, leg, arrived, main, rest, wide, turned, tall, gather):
    for c in range(COLS + 4):
        values = spec[c if c < COLS else c - 4].astype(F32)
        for k in range(8):
            wide[k, c * SLOTS : (c + 1) * SLOTS, :] = values[:, k * 128 : (k + 1) * 128]
    degree = lax.broadcasted_iota(jnp.int32, (40, NM), 1)
    odd = degree % 2 == 1
    lane = lax.broadcasted_iota(jnp.int32, (32, 128), 1)
    turn = lane // 16 % 4
    small = lane // 4 % 4

    def slot(s, j):
        rows = jnp.concatenate(
            [
                jnp.concatenate(
                    [
                        wide[k, pl.ds(s, 16, stride=32), :],
                        wide[k, pl.ds(16 + s, 16, stride=32), :],
                        wide[k, pl.ds(512 + s, 8, stride=16), :],
                    ],
                    axis=0,
                )
                for k in range(8)
            ],
            axis=1,
        )
        rows = jnp.where(degree < NM - numbers(s), rows, 0.0)
        both = jnp.concatenate([rows, jnp.where(odd, -rows, rows)], axis=0).astype(BF)
        sums = dot(both, leg[s])
        for half in range(2):
            own = sums[half * 40 : (half + 1) * 40]
            block = jnp.concatenate([own[0:16]] * 4 + [own[16:32]] * 4, axis=0)
            turned[half, j] = block.T
            lines = [turned[half, j, pl.ds(r, 32, stride=4), :] for r in range(4)]
            if half == 1:
                lines = lines[::-1]
            gather[pl.ds(half * 512 + s, 32, stride=SLOTS), :] = pick(lines, turn)
            tall[half, pl.ds(pl.multiple_of(s * 16, 16), 16), :] = jnp.concatenate(
                [own[32:40]] * 2, axis=0
            )

    def group(i, carry):
        arrived(i)
        for j in range(4):
            slot(4 * i + j, j)
        return carry

    lax.fori_loop(0, 4, group, 0)
    for half in range(2):
        for h in range(2):
            turned[half, h] = tall[half, h * 128 : (h + 1) * 128, :].T
            lines = [turned[half, h, pl.ds(r, 32, stride=4), :] for r in range(4)]
            if half == 1:
                lines = lines[::-1]
            rest[half * 32 : (half + 1) * 32, h, :] = pick(lines, small)
    for b in range(WAVES):
        main[b] = gather[b * SLOTS : (b + 1) * SLOTS, :].astype(BF)


def choose_rows(numbers, choice):
    line = lax.broadcasted_iota(jnp.int32, (32, NM), 0)

    def step(i, carry):
        wanted = i // 4 + RADIX * (i % 4 * 32 + line)
        hit = jnp.where(numbers == wanted, 1.0, 0.0).astype(BF)
        choice[pl.ds(pl.multiple_of(i * 32, 32), 32), :] = hit
        return carry

    lax.fori_loop(0, 32, step, 0)


def fourier_stage(main, rest, choice, order, table, edges, message, small, joined, part, grid, edge):
    joined[:, 0:128] = main[...].reshape(NM, 128)
    for h in range(2):
        values = rest[:, h, :]
        for g in range(8):
            rolled = values if g == 0 else pltpu.roll(values, 128 - 16 * g, 1)
            small[pl.ds(h * 8 + g, WAVES, stride=SLOTS), :] = rolled
    joined[:, 128:256] = small[...].astype(BF)
    ordered = dot(choice[...], joined[...]).astype(BF)
    lines = lax.dot_general(
        order[...], ordered, (((1,), (1,)), ((), ())), preferred_element_type=F32
    )
    for k in range(RADIX):
        own = lines[:, k * 128 : (k + 1) * 128]
        pair = jnp.concatenate([own[0:72].astype(BF), own[72:144].astype(BF)], axis=1)
        part[k] = dot(pair, table[k])
    root = 0.5**0.5

    def combine(i, carry):
        row = pl.ds(pl.multiple_of(i * 8, 8), 8)
        tile = i + jnp.where(i >= EDGE_TILE, 1, 0)
        for h in range(2):
            re = [part[k, row, h * 128 : (h + 1) * 128] for k in range(RADIX)]
            im = [
                None if k % 4 == 0 else part[k, row, SPAN + h * 128 : SPAN + (h + 1) * 128]
                for k in range(RADIX)
            ]
            plus, minus = re[0] + re[4], re[0] - re[4]
            level, cross = re[2] + re[6], im[6] - im[2]
            even = [plus + level, minus + cross, plus - level, minus - cross]
            a, b = re[1] - re[5], re[7] - re[3]
            c, d = im[5] - im[1], im[7] - im[3]
            odd = [
                re[1] + re[3] + re[5] + re[7],
                root * (a + b + c + d),
                im[3] - im[1] + im[7] - im[5],
                root * (c + d - a - b),
            ]
            for u in range(RADIX):
                value = even[u % 4] + odd[u] if u < 4 else even[u % 4] - odd[u - 4]
                message[2 * u + h, tile] = value.astype(BF)
                grid[row, u * SPAN + h * 128 : u * SPAN + (h + 1) * 128] = value
        return carry

    lax.fori_loop(0, 9, combine, 0)
    edge[0:72] = dot(grid[...].astype(BF), edges[...])
    edge[72:80] = jnp.zeros((8, 128), F32)
    lane = lax.broadcasted_iota(jnp.int32, (8, 128), 1) // 8

    def pack(block, carry):
        total = jnp.zeros((8, 128), F32)
        for field in range(3):
            for lat in range(4):
                group, place = PLACE[(field, lat)]
                q = field * 4 + lat
                values = edge[pl.ds(group * 24 + place, 8, stride=4), :]
                rolled = pltpu.roll(values, (128 + 8 * q - 8 * block) % 128, 1)
                total = jnp.where(lane == q, rolled, total)
        message[block, EDGE_TILE] = total.astype(BF)
        return carry

    lax.fori_loop(0, LEVDEV, pack, 0)


def modes_to_levels(sources, edge_sources, both, spread_both, wide, fields, edges):
    for i, ref, tile in sources:
        for d in range(LEVDEV):
            values = ref[d, tile : tile + 3].astype(F32)
            wide[i, d * 24 : (d + 1) * 24, :] = values.reshape(24, 128)
        for q in range(0, 4, 2):
            modes = jnp.concatenate(
                [wide[i, pl.ds(q, LEVS, stride=4), :], wide[i, pl.ds(q + 1, LEVS, stride=4), :]],
                axis=1,
            ).astype(BF)
            twice = dot(both, modes)
            value = twice[:LEVS] + twice[LEVS:]
            fields[i, q] = value[:, :128]
            fields[i, q + 1] = value[:, 128:]
    for i, ref, tile in edge_sources:
        twice = dot(spread_both, ref[:, tile].reshape(128, 128))
        edges[i] = twice[:LEVS] + twice[LEVS:]


def upwind_stage(band, fields, edges, out):
    lane = lax.broadcasted_iota(jnp.int32, (8, 128), 1)
    first, last = band == 0, band == WAVES - 1

    def where_is(field, lat):
        if lat < 0:
            group, place = PLACE[(field, lat + 4)]
            return 3, place
        if lat > 3:
            group, place = PLACE[(field, lat - 4)]
            return 4, place
        return PLACE[(field, lat)]

    def shift(value, amount):
        amount = amount % 128
        return value if amount == 0 else pltpu.roll(value, amount, 1)

    def upwind(center, west, east, north, south, cx, cy):
        return (
            center
            - jnp.maximum(cx, 0.0) * (center - west)
            - jnp.minimum(cx, 0.0) * (east - center)
            - jnp.maximum(cy, 0.0) * (center - north)
            - jnp.minimum(cy, 0.0) * (south - center)
        )

    def line(step, carry):
        level = pl.ds(pl.multiple_of(step * 8, 8), 8)

        def field(f, lat):
            i, q = where_is(f, lat)
            return fields[i, q, level, :]

        def courant(value):
            return COURANT * jnp.tanh(value)

        zero = jnp.zeros((8, 128), F32)
        tracer = {lat: field(2, lat) for lat in range(-2, 6)}
        for lat in (-2, -1):
            tracer[lat] = jnp.where(first, zero, tracer[lat])
        for lat in (4, 5):
            tracer[lat] = jnp.where(last, zero, tracer[lat])
        cx = {lat: courant(field(0, lat)) for lat in range(-1, 5)}
        cy = {lat: courant(field(1, lat)) for lat in range(-1, 5)}
        mine, upper, lower = edges[0, level, :], edges[1, level, :], edges[2, level, :]

        def side(f):
            return jnp.where(
                lane < 16,
                shift(upper, -(f * 32 + 16)),
                jnp.where(lane < 48, shift(mine, 16 - f * 32), shift(lower, 48 - f * 32)),
            )

        edge = side(2)
        edge = jnp.where(((lane < 16) & first) | ((lane >= 48) & last), zero, edge)
        edge_x, edge_y = courant(side(0)), courant(side(1))

        def beside(value, rim, lat):
            west = shift(value, 1)
            west = jnp.where(lane == 0, shift(rim, -((lat + 2) * 8 + 1)), west)
            east = shift(value, -1)
            east = jnp.where(lane == 127, shift(rim, 127 - ((lat + 2) * 8 + 4)), east)
            return west, east

        once = {}
        for lat in range(-1, 5):
            west, east = beside(tracer[lat], edge, lat)
            once[lat] = upwind(
                tracer[lat], west, east, tracer[lat - 1], tracer[lat + 1], cx[lat], cy[lat]
            )
        once[-1] = jnp.where(first, zero, once[-1])
        once[4] = jnp.where(last, zero, once[4])
        rim = upwind(
            edge, shift(edge, 1), shift(edge, -1), shift(edge, 8), shift(edge, -8), edge_x, edge_y
        )
        for lat in range(4):
            west, east = beside(once[lat], rim, lat)
            out[level, lat, :] = upwind(
                once[lat], west, east, once[lat - 1], once[lat + 1], cx[lat], cy[lat]
            )
        return carry

    lax.fori_loop(0, LEVS // 8, line, 0)


def send_rows(w):
    return jnp.where(w < WAVES // 2, w, 95 - w)


def all_in_one(
    numbers_far, line_far, spec_far, leg_far, order_far, table_far, edges_far, vertical_far, spread_far,
    out,
    numbers, line, spec, leg, order, table, edges, vertical, spread,
    load, leg_load,
    wide, turned, tall, gather, main, rest,
    main_in, rest_in, choice, small, joined, part, grid, edge, message,
    own, north, south, modes, fields, rims,
    send, recv, here, halo_send, halo_recv,
):
    w, v = lax.axis_index("wave"), lax.axis_index("lev")
    loads = [
        pltpu.make_async_copy(far, near, load.at[i])
        for i, (far, near) in enumerate(
            (
                (numbers_far, numbers),
                (spec_far, spec),
                (line_far, line),
                (order_far, order),
                (table_far, table),
                (edges_far, edges),
                (vertical_far, vertical),
                (spread_far, spread),
            )
        )
    ]

    def leg_copy(i):
        rows = pl.ds(4 * i, 4)
        return pltpu.make_async_copy(leg_far.at[rows], leg.at[rows], leg_load.at[i])

    for copy in loads[:2]:
        copy.start()
    for i in range(4):
        leg_copy(i).start()
    for copy in loads[2:]:
        copy.start()

    barrier = pltpu.get_barrier_semaphore()

    def greet(axis, count, own_index):
        def step(i, carry):
            other = lax.rem(own_index + i, count)
            pl.semaphore_signal(barrier, inc=1, device_id={axis: other}, device_id_type=MESH)
            return carry

        lax.fori_loop(1, count, step, 0)

    greet("wave", WAVES, w)
    greet("lev", LEVDEV, v)
    loads[0].wait()
    loads[1].wait()
    first = w * SLOTS
    legendre_stage(
        lambda s: numbers[first + s],
        spec, leg, lambda i: leg_copy(i).wait(), main, rest, wide, turned, tall, gather,
    )
    pl.semaphore_wait(barrier, WAVES + LEVDEV - 2)

    pairs = ((main, main_in), (rest, rest_in))

    def to_band(i, carry):
        target = lax.rem(w + i, WAVES)
        row = send_rows(target)
        for j, (src, dst) in enumerate(pairs):
            pltpu.make_async_remote_copy(
                src_ref=src.at[row],
                dst_ref=dst.at[w],
                send_sem=send.at[j],
                recv_sem=recv.at[j],
                device_id={"wave": target},
                device_id_type=MESH,
            ).start()
        return carry

    lax.fori_loop(1, WAVES, to_band, 0)
    row = send_rows(w)
    local = [
        pltpu.make_async_copy(src.at[row], dst.at[w], here.at[j])
        for j, (src, dst) in enumerate(pairs)
    ]
    for copy in local:
        copy.start()
    for copy in loads[2:]:
        copy.wait()
    choose_rows(line[...], choice)
    top = vertical[...].astype(BF)
    low = (vertical[...] - top.astype(F32)).astype(BF)
    both = jnp.concatenate([top, low], axis=0)
    spread_both = dot(both, spread[...]).astype(BF)
    for copy in local:
        copy.wait()
    many = pl.ds(0, WAVES - 1)
    for j, (src, dst) in enumerate(pairs):
        whole = pltpu.make_async_remote_copy(
            src_ref=src.at[many],
            dst_ref=dst.at[many],
            send_sem=send.at[j],
            recv_sem=recv.at[j],
            device_id={"wave": lax.rem(w + 1, WAVES)},
            device_id_type=MESH,
        )
        whole.wait_send()
        whole.wait_recv()

    fourier_stage(
        main_in, rest_in, choice, order, table, edges, message, small, joined, part, grid, edge
    )

    def to_block(i, carry):
        target = lax.rem(v + i, LEVDEV)
        pltpu.make_async_remote_copy(
            src_ref=message.at[target],
            dst_ref=own.at[v],
            send_sem=send.at[2],
            recv_sem=recv.at[2],
            device_id={"lev": target},
            device_id_type=MESH,
        ).start()
        return carry

    lax.fori_loop(1, LEVDEV, to_block, 0)
    local = pltpu.make_async_copy(message.at[v], own.at[v], here.at[2])
    local.start()
    local.wait()
    many = pl.ds(0, LEVDEV - 1)
    whole = pltpu.make_async_remote_copy(
        src_ref=message.at[many],
        dst_ref=own.at[many],
        send_sem=send.at[2],
        recv_sem=recv.at[2],
        device_id={"lev": lax.rem(v + 1, LEVDEV)},
        device_id_type=MESH,
    )
    whole.wait_send()
    whole.wait_recv()
    halos = [
        pltpu.make_async_remote_copy(
            src_ref=own.at[:, tile : tile + 4],
            dst_ref=dst,
            send_sem=halo_send.at[i],
            recv_sem=halo_recv.at[i],
            device_id={"wave": lax.rem(w + step, WAVES)},
            device_id_type=MESH,
        )
        for i, (tile, dst, step) in enumerate(((6, north, 1), (3, south, WAVES - 1)))
    ]
    for copy in halos:
        copy.start()
    modes_to_levels(
        ((0, own, 0), (1, own, 3), (2, own, 7)),
        ((0, own, EDGE_TILE),),
        both, spread_both, modes, fields, rims,
    )
    for copy in halos:
        copy.wait()
    modes_to_levels(
        ((3, north, 1), (4, south, 0)),
        ((1, north, 0), (2, south, 3)),
        both, spread_both, modes, fields, rims,
    )
    upwind_stage(w, fields, rims, out)


def body(spectrum, legendre, wave_numbers, vertical):
    spec = jnp.transpose(spectrum, (2, 3, 0, 1)).reshape(COLS, SLOTS, NM)
    dma = pltpu.SemaphoreType.DMA
    far = pl.BlockSpec(memory_space=pl.ANY)
    near = pltpu.VMEM
    message = (LEVDEV, 10, 8, 128)
    halo = (LEVDEV, 4, 8, 128)
    return pl.pallas_call(
        all_in_one,
        name="synthesis",
        out_shape=jax.ShapeDtypeStruct((LEVS, 4, 128), F32),
        in_specs=[far] * 9,
        out_specs=pl.BlockSpec(memory_space=near),
        scratch_shapes=[
            pltpu.SMEM((NM,), jnp.int32),
            near((1, NM), jnp.int32),
            near((COLS, SLOTS, NM), BF),
            near((SLOTS, NM, 128), BF),
            near((144, 256), BF),
            near((RADIX, 256, 2 * SPAN), BF),
            near((NLON, 128), BF),
            near((LEVS, LEVS), F32),
            near((LEVS, 128), BF),
            dma((8,)),
            dma((4,)),
            near((8, 640, 128), F32),
            near((2, 4, 128, 128), F32),
            near((2, 256, 128), F32),
            near((WAVES * SLOTS, 128), F32),
            near((WAVES, SLOTS, 128), BF),
            near((WAVES, 2, 128), F32),
            near((WAVES, SLOTS, 128), BF),
            near((WAVES, 2, 128), F32),
            near((NM, NM), BF),
            near((NM, 128), F32),
            near((NM, 256), BF),
            near((RADIX, 72, 2 * SPAN), F32),
            near((72, NLON), F32),
            near((80, 128), F32),
            near(message, BF),
            near(message, BF),
            near(halo, BF),
            near(halo, BF),
            near((5, LEVDEV * 24, 128), F32),
            near((5, 4, LEVS, 128), F32),
            near((3, LEVS, 128), F32),
            dma((3,)),
            dma((3,)),
            dma((3,)),
            dma((2,)),
            dma((2,)),
        ],
        compiler_params=pltpu.CompilerParams(
            vmem_limit_bytes=60 * 2**20, collective_id=0, has_side_effects=True
        ),
    )(
        wave_numbers,
        wave_numbers.reshape(1, NM),
        spec,
        legendre,
        jnp.asarray(row_table()),
        jnp.asarray(fourier_table()),
        jnp.asarray(edge_table()),
        vertical,
        jnp.asarray(spread_table()),
    )


def solution(mesh):
    placed = (P("wave", None, "lev", None), P("wave", None, None), P(), P())
    return jax.shard_map(
        body, mesh=mesh, in_specs=placed, out_specs=P(None, "wave", "lev"), check_vma=False
    )
```

```python
import jax
import jax.numpy as jnp
import numpy as np
from jax import lax
from jax.experimental import pallas as pl
from jax.experimental.pallas import tpu as pltpu
from jax.sharding import PartitionSpec as P

BF = jnp.bfloat16
F32 = jnp.float32
MESH = pl.DeviceIdType.MESH
COURANT = 0.45

NM = 1024
NLON = 2048
LEVS = 96
WAVES = 64
LEVDEV = 16
SLOTS = 16
COLS = 36
MODES = 6
RADIX = 8
SPAN = NLON // RADIX

GROUPS = (
    ((0, 1), (1, 1), (0, 2), (1, 2)),
    ((0, 0), (1, 0), (2, 0), (2, 1)),
    ((2, 2), (2, 3), (1, 3), (0, 3)),
)
PLACE = {pair: (g, i) for g, group in enumerate(GROUPS) for i, pair in enumerate(group)}
EDGE_TILE = 6
OFFSETS = (-2, -1, 0, 127, 128, 129)


def fourier_table():
    numbers = np.arange(NM).reshape(NM // RADIX, RADIX).T
    residue = numbers[:, :, None] * np.arange(SPAN)[None, None, :] % NLON
    angle = residue * (2.0 * np.pi / NLON)
    weight = np.where(numbers == 0, 1.0, 2.0)[:, :, None]
    real, imaginary = weight * np.cos(angle), weight * np.sin(angle)
    imaginary = np.where(residue == 0, 0.0, imaginary)
    top = np.concatenate([real, imaginary], axis=2)
    bottom = np.concatenate([-imaginary, real], axis=2)
    return np.concatenate([top, bottom], axis=1).astype(BF)


def row_table():
    table = np.zeros((144, 256), np.float32)
    for (field, lat), (group, place) in PLACE.items():
        for mode in range(MODES):
            for part in range(2):
                pair = mode * 3 + field
                if pair < 16:
                    column = part * 64 + lat * 16 + pair
                else:
                    column = 128 + lat * 4 + (pair - 16) * 2 + part
                table[part * 72 + group * 24 + mode * 4 + place, column] = 1.0
    return table.astype(BF)


def edge_table():
    table = np.zeros((NLON, 128), np.float32)
    for block in range(LEVDEV):
        for k, offset in enumerate(OFFSETS):
            table[(block * 128 + offset) % NLON, block * 8 + k] = 1.0
    return table.astype(BF)


def spread_table():
    table = np.zeros((LEVS, 128), np.float32)
    for mode in range(LEVS):
        table[mode, mode // MODES * 8 + mode % MODES] = 1.0
    return table.astype(BF)


def dot(a, b):
    return jnp.dot(a, b, preferred_element_type=F32)


def pick(values, index):
    result = values[-1]
    for i in range(len(values) - 2, -1, -1):
        result = jnp.where(index == i, values[i], result)
    return result


def legendre_stage(numbers, spec, leg, arrived, main, rest, wide, turned, tall, gather):
    for c in range(COLS + 4):
        values = spec[c if c < COLS else c - 4].astype(F32)
        for k in range(8):
            wide[k, c * SLOTS : (c + 1) * SLOTS, :] = values[:, k * 128 : (k + 1) * 128]
    degree = lax.broadcasted_iota(jnp.int32, (40, NM), 1)
    odd = degree % 2 == 1
    lane = lax.broadcasted_iota(jnp.int32, (32, 128), 1)
    turn = lane // 16 % 4
    small = lane // 4 % 4

    def slot(s, j):
        rows = jnp.concatenate(
            [
                jnp.concatenate(
                    [
                        wide[k, pl.ds(s, 16, stride=32), :],
                        wide[k, pl.ds(16 + s, 16, stride=32), :],
                        wide[k, pl.ds(512 + s, 8, stride=16), :],
                    ],
                    axis=0,
                )
                for k in range(8)
            ],
            axis=1,
        )
        rows = jnp.where(degree < NM - numbers(s), rows, 0.0)
        both = jnp.concatenate([rows, jnp.where(odd, -rows, rows)], axis=0).astype(BF)
        sums = dot(both, leg[s])
        for half in range(2):
            own = sums[half * 40 : (half + 1) * 40]
            block = jnp.concatenate([own[0:16]] * 4 + [own[16:32]] * 4, axis=0)
            turned[half, j] = block.T
            lines = [turned[half, j, pl.ds(r, 32, stride=4), :] for r in range(4)]
            if half == 1:
                lines = lines[::-1]
            gather[pl.ds(half * 512 + s, 32, stride=SLOTS), :] = pick(lines, turn)
            tall[half, pl.ds(pl.multiple_of(s * 16, 16), 16), :] = jnp.concatenate(
                [own[32:40]] * 2, axis=0
            )

    def group(i, carry):
        arrived(i)
        for j in range(4):
            slot(4 * i + j, j)
        return carry

    lax.fori_loop(0, 4, group, 0)
    for half in range(2):
        for h in range(2):
            turned[half, h] = tall[half, h * 128 : (h + 1) * 128, :].T
            lines = [turned[half, h, pl.ds(r, 32, stride=4), :] for r in range(4)]
            if half == 1:
                lines = lines[::-1]
            if half == 0:
                rest[0:32, h, :] = pick(lines, small)
            else:
                chosen = pick(lines, small)
                for b in range(32):
                    rest[WAVES - 1 - b, h : h + 1, :] = chosen[b : b + 1]
    for b in range(WAVES):
        band = b if b < 32 else 95 - b
        main[band] = gather[b * SLOTS : (b + 1) * SLOTS, :].astype(BF)


def choose_rows(numbers, choice):
    line = lax.broadcasted_iota(jnp.int32, (32, NM), 0)

    def step(i, carry):
        wanted = i // 4 + RADIX * (i % 4 * 32 + line)
        hit = jnp.where(numbers == wanted, 1.0, 0.0).astype(BF)
        choice[pl.ds(pl.multiple_of(i * 32, 32), 32), :] = hit
        return carry

    lax.fori_loop(0, 32, step, 0)


def fourier_stage(main, rest, choice, order, table, edges, message, small, joined, part, grid, edge, ready):
    joined[:, 0:128] = main[...].reshape(NM, 128)
    for h in range(2):
        values = rest[:, h, :]
        for g in range(8):
            rolled = values if g == 0 else pltpu.roll(values, 128 - 16 * g, 1)
            small[pl.ds(h * 8 + g, WAVES, stride=SLOTS), :] = rolled
    joined[:, 128:256] = small[...].astype(BF)
    ordered = dot(choice[...], joined[...]).astype(BF)
    lines = lax.dot_general(
        order[...], ordered, (((1,), (1,)), ((), ())), preferred_element_type=F32
    )
    for k in range(RADIX):
        own = lines[:, k * 128 : (k + 1) * 128]
        pair = jnp.concatenate([own[0:72].astype(BF), own[72:144].astype(BF)], axis=1)
        part[k] = dot(pair, table[k])
    root = 0.5**0.5

    def combine(i, carry):
        row = pl.ds(pl.multiple_of(i * 8, 8), 8)
        tile = i + jnp.where(i >= EDGE_TILE, 1, 0)
        for h in range(2):
            re = [part[k, row, h * 128 : (h + 1) * 128] for k in range(RADIX)]
            im = [
                None if k % 4 == 0 else part[k, row, SPAN + h * 128 : SPAN + (h + 1) * 128]
                for k in range(RADIX)
            ]
            plus, minus = re[0] + re[4], re[0] - re[4]
            level, cross = re[2] + re[6], im[6] - im[2]
            even = [plus + level, minus + cross, plus - level, minus - cross]
            a, b = re[1] - re[5], re[7] - re[3]
            c, d = im[5] - im[1], im[7] - im[3]
            odd = [
                re[1] + re[3] + re[5] + re[7],
                root * (a + b + c + d),
                im[3] - im[1] + im[7] - im[5],
                root * (c + d - a - b),
            ]
            for u in range(RADIX):
                value = even[u % 4] + odd[u] if u < 4 else even[u % 4] - odd[u - 4]
                message[2 * u + h, tile] = value.astype(BF)
                grid[row, u * SPAN + h * 128 : u * SPAN + (h + 1) * 128] = value
        return carry

    lax.fori_loop(0, 3, combine, 0)
    ready(0, 3)
    lax.fori_loop(3, 6, combine, 0)
    ready(3, 3)
    lax.fori_loop(6, 9, combine, 0)
    edge[0:72] = dot(grid[...].astype(BF), edges[...])
    edge[72:80] = jnp.zeros((8, 128), F32)
    lane = lax.broadcasted_iota(jnp.int32, (8, 128), 1) // 8

    def pack(block, carry):
        total = jnp.zeros((8, 128), F32)
        for field in range(3):
            for lat in range(4):
                group, place = PLACE[(field, lat)]
                q = field * 4 + lat
                values = edge[pl.ds(group * 24 + place, 8, stride=4), :]
                rolled = pltpu.roll(values, (128 + 8 * q - 8 * block) % 128, 1)
                total = jnp.where(lane == q, rolled, total)
        message[block, EDGE_TILE] = total.astype(BF)
        return carry

    lax.fori_loop(0, LEVDEV, pack, 0)
    ready(6, 4)


def modes_to_levels(groups, both, wide, fields):
    for i in groups:
        for q in range(0, 4, 2):
            modes = jnp.concatenate(
                [wide[i, pl.ds(q, LEVS, stride=4), :], wide[i, pl.ds(q + 1, LEVS, stride=4), :]],
                axis=1,
            ).astype(BF)
            twice = dot(both, modes)
            value = twice[:LEVS] + twice[LEVS:]
            fields[i, q] = value[:, :128]
            fields[i, q + 1] = value[:, 128:]


def rims_of(sources, spread_both, rims):
    for i, ref, tile in sources:
        twice = dot(spread_both, ref[:, tile].reshape(128, 128))
        rims[i] = twice[:LEVS] + twice[LEVS:]


def upwind_stage(band, fields, edges, out, change):
    lane = lax.broadcasted_iota(jnp.int32, (8, 128), 1)
    first, last = band == 0, band == WAVES - 1

    def where_is(field, lat):
        if lat < 0:
            group, place = PLACE[(field, lat + 4)]
            return 3, place
        if lat > 3:
            group, place = PLACE[(field, lat - 4)]
            return 4, place
        return PLACE[(field, lat)]

    def shift(value, amount):
        amount = amount % 128
        return value if amount == 0 else pltpu.roll(value, amount, 1)

    def upwind(center, west, east, north, south, cx, cy):
        return (
            center
            - jnp.maximum(cx, 0.0) * (center - west)
            - jnp.minimum(cx, 0.0) * (east - center)
            - jnp.maximum(cy, 0.0) * (center - north)
            - jnp.minimum(cy, 0.0) * (south - center)
        )

    def line(step, carry):
        level = pl.ds(pl.multiple_of(step * 8, 8), 8)

        def field(f, lat):
            i, q = where_is(f, lat)
            return fields[i, q, level, :]

        def courant(value):
            return COURANT * jnp.tanh(value)

        zero = jnp.zeros((8, 128), F32)
        tracer = {lat: field(2, lat) for lat in range(-2, 6)}
        for lat in (-2, -1):
            tracer[lat] = jnp.where(first, zero, tracer[lat])
        for lat in (4, 5):
            tracer[lat] = jnp.where(last, zero, tracer[lat])
        cx = {lat: courant(field(0, lat)) for lat in range(-1, 5)}
        cy = {lat: courant(field(1, lat)) for lat in range(-1, 5)}
        mine, upper, lower = edges[0, level, :], edges[1, level, :], edges[2, level, :]

        def side(f):
            return jnp.where(
                lane < 16,
                shift(upper, -(f * 32 + 16)),
                jnp.where(lane < 48, shift(mine, 16 - f * 32), shift(lower, 48 - f * 32)),
            )

        edge = side(2)
        edge = jnp.where(((lane < 16) & first) | ((lane >= 48) & last), zero, edge)
        edge_x, edge_y = courant(side(0)), courant(side(1))

        def beside(value, rim, lat):
            west = shift(value, 1)
            west = jnp.where(lane == 0, shift(rim, -((lat + 2) * 8 + 1)), west)
            east = shift(value, -1)
            east = jnp.where(lane == 127, shift(rim, 127 - ((lat + 2) * 8 + 4)), east)
            return west, east

        once = {}
        for lat in range(-1, 5):
            west, east = beside(tracer[lat], edge, lat)
            once[lat] = upwind(
                tracer[lat], west, east, tracer[lat - 1], tracer[lat + 1], cx[lat], cy[lat]
            )
        once[-1] = jnp.where(first, zero, once[-1])
        once[4] = jnp.where(last, zero, once[4])
        rim = upwind(
            edge, shift(edge, 1), shift(edge, -1), shift(edge, 8), shift(edge, -8), edge_x, edge_y
        )
        for lat in range(4):
            west, east = beside(once[lat], rim, lat)
            row = pl.ds(step * 32 + lat, 8, stride=4)
            out[row, :] = once[lat]
            change[row, :] = (
                jnp.maximum(cx[lat], 0.0) * (once[lat] - west)
                + jnp.minimum(cx[lat], 0.0) * (east - once[lat])
                + jnp.maximum(cy[lat], 0.0) * (once[lat] - once[lat - 1])
                + jnp.minimum(cy[lat], 0.0) * (once[lat + 1] - once[lat])
            )
        return carry

    lax.fori_loop(0, LEVS // 8, line, 0)


def all_in_one(
    numbers_far, line_far, spec_far, leg_far, order_far, table_far, edges_far, vertical_far, spread_far,
    out, change,
    numbers, line, spec, leg, order, table, edges, vertical, spread,
    load, leg_load,
    wide, turned, tall, gather, main, rest,
    main_in, rest_in, choice, small, joined, part, grid, edge, message,
    own, north, south, modes, fields, rims,
    send, recv, here, block_recv, halo_send, halo_recv,
):
    w, v = lax.axis_index("wave"), lax.axis_index("lev")
    loads = [
        pltpu.make_async_copy(far, near, load.at[i])
        for i, (far, near) in enumerate(
            (
                (numbers_far, numbers),
                (spec_far, spec),
                (line_far, line),
                (order_far, order),
                (table_far, table),
                (edges_far, edges),
                (vertical_far, vertical),
                (spread_far, spread),
            )
        )
    ]

    def leg_copy(i):
        rows = pl.ds(4 * i, 4)
        return pltpu.make_async_copy(leg_far.at[rows], leg.at[rows], leg_load.at[i])

    for copy in loads[:2]:
        copy.start()
    for i in range(4):
        leg_copy(i).start()
    for copy in loads[2:]:
        copy.start()

    barrier = pltpu.get_barrier_semaphore()

    def greet(axis, count, own_index):
        def step(i, carry):
            other = lax.rem(own_index + i, count)
            pl.semaphore_signal(barrier, inc=1, device_id={axis: other}, device_id_type=MESH)
            return carry

        lax.fori_loop(1, count, step, 0)

    greet("wave", WAVES, w)
    greet("lev", LEVDEV, v)
    loads[0].wait()
    loads[1].wait()
    first = w * SLOTS
    legendre_stage(
        lambda s: numbers[first + s],
        spec, leg, lambda i: leg_copy(i).wait(), main, rest, wide, turned, tall, gather,
    )
    pl.semaphore_wait(barrier, WAVES + LEVDEV - 2)

    pairs = ((main, main_in), (rest, rest_in))

    def to_band(i, carry):
        target = w + i
        target = jnp.where(target >= WAVES, target - WAVES, target)
        for j, (src, dst) in enumerate(pairs):
            pltpu.make_async_remote_copy(
                src_ref=src.at[target],
                dst_ref=dst.at[w],
                send_sem=send.at[j],
                recv_sem=recv.at[j],
                device_id={"wave": target},
                device_id_type=MESH,
            ).start()
        return carry

    lax.fori_loop(1, WAVES, to_band, 0, unroll=9)
    local = [
        pltpu.make_async_copy(src.at[w], dst.at[w], here.at[j])
        for j, (src, dst) in enumerate(pairs)
    ]
    for copy in local:
        copy.start()
    for copy in loads[2:]:
        copy.wait()
    choose_rows(line[...], choice)
    top = vertical[...].astype(BF)
    low = (vertical[...] - top.astype(F32)).astype(BF)
    both = jnp.concatenate([top, low], axis=0)
    spread_both = dot(both, spread[...]).astype(BF)
    for copy in local:
        copy.wait()
    many = pl.ds(0, WAVES - 1)
    for j, (src, dst) in enumerate(pairs):
        whole = pltpu.make_async_remote_copy(
            src_ref=src.at[many],
            dst_ref=dst.at[many],
            send_sem=send.at[j],
            recv_sem=recv.at[j],
            device_id={"wave": lax.rem(w + 1, WAVES)},
            device_id_type=MESH,
        )
        whole.wait_send()
        whole.wait_recv()

    shifts = [8] + [8 + sign * k for k in range(1, 8) for sign in (-1, 1)]

    def other_block(shift):
        block = v + shift
        return jnp.where(block >= LEVDEV, block - LEVDEV, block)

    def block_copy(src, dst, shift):
        return pltpu.make_async_remote_copy(
            src_ref=message.at[other_block(shift)] if src is None else src,
            dst_ref=dst,
            send_sem=send.at[2],
            recv_sem=block_recv.at[v],
            device_id={"lev": other_block(shift)},
            device_id_type=MESH,
        )

    def ready(tile, count):
        rows = pl.ds(tile, count)
        for shift in shifts:
            block_copy(
                message.at[other_block(shift), rows], own.at[v, rows], shift
            ).start()

    fourier_stage(
        main_in, rest_in, choice, order, table, edges, message, small, joined, part, grid, edge, ready
    )
    itself = pltpu.make_async_copy(message.at[v], own.at[v], here.at[2])
    itself.start()
    itself.wait()

    def halo_copy(i, src, dst):
        return pltpu.make_async_remote_copy(
            src_ref=src,
            dst_ref=dst,
            send_sem=halo_send.at[i],
            recv_sem=halo_recv.at[i],
            device_id={"wave": lax.rem(w + (1 if i == 0 else WAVES - 1), WAVES)},
            device_id_type=MESH,
        )

    def pass_on(block):
        halo_copy(0, own.at[block, pl.ds(6, 4)], north.at[block]).start()
        halo_copy(1, own.at[block, pl.ds(3, 4)], south.at[block]).start()
        row = pl.ds(pl.multiple_of(block * 24, 8), 24)
        for i, tile in enumerate((0, 3, 7)):
            modes[i, row, :] = own[block, tile : tile + 3].astype(F32).reshape(24, 128)

    pass_on(v)
    for shift in shifts:
        block = other_block(LEVDEV - shift)
        pltpu.make_async_remote_copy(
            src_ref=message.at[block],
            dst_ref=own.at[block],
            send_sem=send.at[2],
            recv_sem=block_recv.at[block],
            device_id={"lev": block},
            device_id_type=MESH,
        ).wait_recv()
        pass_on(block)
    modes_to_levels((0, 1, 2), both, modes, fields)
    rims_of(((0, own, EDGE_TILE),), spread_both, rims)
    many = pl.ds(0, LEVDEV - 1)
    block_copy(message.at[many], own.at[many], 1).wait_send()
    halo_copy(0, own.at[:, pl.ds(6, 4)], north).wait()
    halo_copy(1, own.at[:, pl.ds(3, 4)], south).wait()
    for i, ref, tile in ((3, north, 1), (4, south, 0)):
        for d in range(LEVDEV):
            modes[i, d * 24 : (d + 1) * 24, :] = ref[d, tile : tile + 3].astype(F32).reshape(24, 128)
    modes_to_levels((3, 4), both, modes, fields)
    rims_of(((1, north, 0), (2, south, 3)), spread_both, rims)
    upwind_stage(w, fields, rims, out, change)


def body(spectrum, legendre, wave_numbers, vertical):
    spec = jnp.transpose(spectrum, (2, 3, 0, 1)).reshape(COLS, SLOTS, NM)
    dma = pltpu.SemaphoreType.DMA
    far = pl.BlockSpec(memory_space=pl.ANY)
    near = pltpu.VMEM
    here = pl.BlockSpec(memory_space=pltpu.VMEM)
    message = (LEVDEV, 10, 8, 128)
    halo = (LEVDEV, 4, 8, 128)
    before, change = pl.pallas_call(
        all_in_one,
        name="synthesis",
        out_shape=(jax.ShapeDtypeStruct((LEVS * 4, 128), F32),) * 2,
        in_specs=[far] * 9,
        out_specs=(here, here),
        scratch_shapes=[
            pltpu.SMEM((NM,), jnp.int32),
            near((1, NM), jnp.int32),
            near((COLS, SLOTS, NM), BF),
            near((SLOTS, NM, 128), BF),
            near((144, 256), BF),
            near((RADIX, 256, 2 * SPAN), BF),
            near((NLON, 128), BF),
            near((LEVS, LEVS), F32),
            near((LEVS, 128), BF),
            dma((8,)),
            dma((4,)),
            near((8, 640, 128), F32),
            near((2, 4, 128, 128), F32),
            near((2, 256, 128), F32),
            near((WAVES * SLOTS, 128), F32),
            near((WAVES, SLOTS, 128), BF),
            near((WAVES, 2, 128), F32),
            near((WAVES, SLOTS, 128), BF),
            near((WAVES, 2, 128), F32),
            near((NM, NM), BF),
            near((NM, 128), F32),
            near((NM, 256), BF),
            near((RADIX, 72, 2 * SPAN), F32),
            near((72, NLON), F32),
            near((80, 128), F32),
            near(message, BF),
            near(message, BF),
            near(halo, BF),
            near(halo, BF),
            near((5, LEVDEV * 24, 128), F32),
            near((5, 4, LEVS, 128), F32),
            near((3, LEVS, 128), F32),
            dma((3,)),
            dma((2,)),
            dma((3,)),
            dma((LEVDEV,)),
            dma((2,)),
            dma((2,)),
        ],
        compiler_params=pltpu.CompilerParams(
            vmem_limit_bytes=60 * 2**20, collective_id=0, has_side_effects=True
        ),
    )(
        wave_numbers,
        wave_numbers.reshape(1, NM),
        spec,
        legendre,
        jnp.asarray(row_table()),
        jnp.asarray(fourier_table()),
        jnp.asarray(edge_table()),
        vertical,
        jnp.asarray(spread_table()),
    )
    return (before - change).reshape(LEVS, 4, 128)


def solution(mesh):
    placed = (P("wave", None, "lev", None), P("wave", None, None), P(), P())
    return jax.shard_map(
        body, mesh=mesh, in_specs=placed, out_specs=P(None, "wave", "lev"), check_vma=False
    )
```

```python
import jax
import jax.numpy as jnp
import numpy as np
from jax import lax
from jax.experimental import pallas as pl
from jax.experimental.pallas import tpu as pltpu
from jax.sharding import PartitionSpec as P

BF = jnp.bfloat16
F32 = jnp.float32
MESH = pl.DeviceIdType.MESH
COURANT = 0.45

NM = 1024
NLON = 2048
LEVS = 96
WAVES = 64
LEVDEV = 16
SLOTS = 16
COLS = 36
MODES = 6
RADIX = 8
SPAN = NLON // RADIX

GROUPS = (
    ((0, 1), (1, 1), (0, 2), (1, 2)),
    ((0, 0), (1, 0), (2, 0), (2, 1)),
    ((2, 2), (2, 3), (1, 3), (0, 3)),
)
PLACE = {pair: (g, i) for g, group in enumerate(GROUPS) for i, pair in enumerate(group)}
EDGE_TILE = 6
OFFSETS = (-2, -1, 0, 127, 128, 129)


def fourier_table():
    numbers = np.arange(NM).reshape(NM // RADIX, RADIX).T
    residue = numbers[:, :, None] * np.arange(SPAN)[None, None, :] % NLON
    angle = residue * (2.0 * np.pi / NLON)
    weight = np.where(numbers == 0, 1.0, 2.0)[:, :, None]
    real, imaginary = weight * np.cos(angle), weight * np.sin(angle)
    imaginary = np.where(residue == 0, 0.0, imaginary)
    top = np.concatenate([real, imaginary], axis=2)
    bottom = np.concatenate([-imaginary, real], axis=2)
    return np.concatenate([top, bottom], axis=1).astype(BF)


def row_table():
    table = np.zeros((144, 256), np.float32)
    for (field, lat), (group, place) in PLACE.items():
        for mode in range(MODES):
            for part in range(2):
                pair = mode * 3 + field
                if pair < 16:
                    column = part * 64 + lat * 16 + pair
                else:
                    column = 128 + lat * 4 + (pair - 16) * 2 + part
                table[part * 72 + group * 24 + mode * 4 + place, column] = 1.0
    return table.astype(BF)


def edge_table():
    table = np.zeros((NLON, 128), np.float32)
    for block in range(LEVDEV):
        for k, offset in enumerate(OFFSETS):
            table[(block * 128 + offset) % NLON, block * 8 + k] = 1.0
    return table.astype(BF)


def spread_table():
    table = np.zeros((LEVS, 128), np.float32)
    for mode in range(LEVS):
        table[mode, mode // MODES * 8 + mode % MODES] = 1.0
    return table.astype(BF)


def dot(a, b):
    return jnp.dot(a, b, preferred_element_type=F32)


def pick(values, index):
    result = values[-1]
    for i in range(len(values) - 2, -1, -1):
        result = jnp.where(index == i, values[i], result)
    return result


def legendre_stage(numbers, spec, leg, arrived, main, rest, wide, turned, tall, gather):
    rest[...] = jnp.zeros_like(rest)
    for c in range(COLS + 4):
        values = spec[c if c < COLS else c - 4].astype(F32)
        for k in range(8):
            wide[k, c * SLOTS : (c + 1) * SLOTS, :] = values[:, k * 128 : (k + 1) * 128]
    degree = lax.broadcasted_iota(jnp.int32, (1, NM), 1)
    sign = jnp.where(degree % 2 == 1, -1.0, 1.0)
    lane = lax.broadcasted_iota(jnp.int32, (32, 128), 1)
    turn = lane // 16 % 4
    small = lane // 4 % 4

    def slot(s, j):
        rows = jnp.concatenate(
            [
                jnp.concatenate(
                    [
                        wide[k, pl.ds(s, 16, stride=32), :],
                        wide[k, pl.ds(16 + s, 16, stride=32), :],
                        wide[k, pl.ds(512 + s, 8, stride=16), :],
                    ],
                    axis=0,
                )
                for k in range(8)
            ],
            axis=1,
        )
        counted = jnp.where(degree < NM - numbers(s), 1.0, 0.0)
        both = jnp.concatenate([rows * counted, rows * (counted * sign)], axis=0).astype(BF)
        sums = dot(both, leg[s])
        for half in range(2):
            own = sums[half * 40 : (half + 1) * 40]
            block = jnp.concatenate([own[0:16]] * 4 + [own[16:32]] * 4, axis=0)
            turned[half, j] = block.T
            lines = [turned[half, j, pl.ds(r, 32, stride=4), :] for r in range(4)]
            if half == 1:
                lines = lines[::-1]
            gather[pl.ds(half * 512 + s, 32, stride=SLOTS), :] = pick(lines, turn)
            tall[half, pl.ds(pl.multiple_of(s * 16, 16), 16), :] = jnp.concatenate(
                [own[32:40]] * 2, axis=0
            )

    def group(i, carry):
        arrived(i)
        for j in range(4):
            slot(4 * i + j, j)
        return carry

    lax.fori_loop(0, 4, group, 0)
    for half in range(2):
        for h in range(2):
            turned[half, h] = tall[half, h * 128 : (h + 1) * 128, :].T
            lines = [turned[half, h, pl.ds(r, 32, stride=4), :] for r in range(4)]
            if half == 1:
                lines = lines[::-1]
            rest[pl.ds(half * 256 + h, 32, stride=8), :] = pick(lines, small)
    for b in range(WAVES):
        band = b if b < 32 else 95 - b
        main[band, 0:2] = gather[b * SLOTS : (b + 1) * SLOTS, :].astype(BF).reshape(2, 8, 128)
        main[band, 2] = rest[b * 8 : (b + 1) * 8, :].astype(BF)


def choose_rows(numbers, choice):
    line = lax.broadcasted_iota(jnp.int32, (32, NM), 0)

    def step(i, carry):
        wanted = i // 4 + RADIX * (i % 4 * 32 + line)
        hit = jnp.where(numbers == wanted, 1.0, 0.0).astype(BF)
        choice[pl.ds(pl.multiple_of(i * 32, 32), 32), :] = hit
        return carry

    lax.fori_loop(0, 32, step, 0)


def fourier_stage(main, rest, choice, order, table, edges, message, small, joined, part, grid, edge, ready):
    joined[:, 0:128] = main[:, 0:2].reshape(NM, 128)
    for i in range(8):
        tiles = main[i * 8 : (i + 1) * 8, 2].astype(F32)
        rest[i * 64 : (i + 1) * 64, :] = tiles.reshape(64, 128)
    for h in range(2):
        values = rest[pl.ds(h, WAVES, stride=8), :]
        for g in range(8):
            rolled = values if g == 0 else pltpu.roll(values, 128 - 16 * g, 1)
            small[pl.ds(h * 8 + g, WAVES, stride=SLOTS), :] = rolled
    joined[:, 128:256] = small[...].astype(BF)
    ordered = dot(choice[...], joined[...]).astype(BF)
    lines = lax.dot_general(
        order[...], ordered, (((1,), (1,)), ((), ())), preferred_element_type=F32
    )
    for k in range(RADIX):
        own = lines[:, k * 128 : (k + 1) * 128]
        pair = jnp.concatenate([own[0:72].astype(BF), own[72:144].astype(BF)], axis=1)
        part[k] = dot(pair, table[k])
    root = 0.5**0.5

    def combine(i, carry):
        row = pl.ds(pl.multiple_of(i * 8, 8), 8)
        tile = i + jnp.where(i >= EDGE_TILE, 1, 0)
        for h in range(2):
            re = [part[k, row, h * 128 : (h + 1) * 128] for k in range(RADIX)]
            im = [
                None if k % 4 == 0 else part[k, row, SPAN + h * 128 : SPAN + (h + 1) * 128]
                for k in range(RADIX)
            ]
            plus, minus = re[0] + re[4], re[0] - re[4]
            level, cross = re[2] + re[6], im[6] - im[2]
            even = [plus + level, minus + cross, plus - level, minus - cross]
            a, b = re[1] - re[5], re[7] - re[3]
            c, d = im[5] - im[1], im[7] - im[3]
            odd = [
                re[1] + re[3] + re[5] + re[7],
                root * (a + b + c + d),
                im[3] - im[1] + im[7] - im[5],
                root * (c + d - a - b),
            ]
            for u in range(RADIX):
                value = even[u % 4] + odd[u] if u < 4 else even[u % 4] - odd[u - 4]
                message[2 * u + h, tile] = value.astype(BF)
                grid[row, u * SPAN + h * 128 : u * SPAN + (h + 1) * 128] = value
        return carry

    lax.fori_loop(0, 3, combine, 0)
    ready(0, 3)
    lax.fori_loop(3, 6, combine, 0)
    ready(3, 3)
    lax.fori_loop(6, 9, combine, 0)
    edge[0:72] = dot(grid[...].astype(BF), edges[...])
    edge[72:80] = jnp.zeros((8, 128), F32)
    lane = lax.broadcasted_iota(jnp.int32, (8, 128), 1) // 8

    def pack(block, carry):
        total = jnp.zeros((8, 128), F32)
        for field in range(3):
            for lat in range(4):
                group, place = PLACE[(field, lat)]
                q = field * 4 + lat
                values = edge[pl.ds(group * 24 + place, 8, stride=4), :]
                rolled = pltpu.roll(values, (128 + 8 * q - 8 * block) % 128, 1)
                total = jnp.where(lane == q, rolled, total)
        message[block, EDGE_TILE] = total.astype(BF)
        return carry

    lax.fori_loop(0, LEVDEV, pack, 0)
    ready(6, 4)


def modes_to_levels(groups, both, wide, fields):
    for i in groups:
        for q in range(0, 4, 2):
            modes = jnp.concatenate(
                [wide[i, pl.ds(q, LEVS, stride=4), :], wide[i, pl.ds(q + 1, LEVS, stride=4), :]],
                axis=1,
            ).astype(BF)
            twice = dot(both, modes)
            value = twice[:LEVS] + twice[LEVS:]
            fields[i, q] = value[:, :128]
            fields[i, q + 1] = value[:, 128:]


def rims_of(sources, spread_both, rims):
    for i, ref, tile in sources:
        twice = dot(spread_both, ref[:, tile].reshape(128, 128))
        rims[i] = twice[:LEVS] + twice[LEVS:]


def upwind_stage(band, fields, edges, out, change):
    lane = lax.broadcasted_iota(jnp.int32, (8, 128), 1)
    first, last = band == 0, band == WAVES - 1

    def where_is(field, lat):
        if lat < 0:
            group, place = PLACE[(field, lat + 4)]
            return 3, place
        if lat > 3:
            group, place = PLACE[(field, lat - 4)]
            return 4, place
        return PLACE[(field, lat)]

    def shift(value, amount):
        amount = amount % 128
        return value if amount == 0 else pltpu.roll(value, amount, 1)

    def upwind(center, west, east, north, south, cx, cy):
        return (
            center
            - jnp.maximum(cx, 0.0) * (center - west)
            - jnp.minimum(cx, 0.0) * (east - center)
            - jnp.maximum(cy, 0.0) * (center - north)
            - jnp.minimum(cy, 0.0) * (south - center)
        )

    def line(step, carry):
        level = pl.ds(pl.multiple_of(step * 8, 8), 8)

        def field(f, lat):
            i, q = where_is(f, lat)
            return fields[i, q, level, :]

        def courant(value):
            return COURANT * jnp.tanh(value)

        zero = jnp.zeros((8, 128), F32)
        tracer = {lat: field(2, lat) for lat in range(-2, 6)}
        for lat in (-2, -1):
            tracer[lat] = jnp.where(first, zero, tracer[lat])
        for lat in (4, 5):
            tracer[lat] = jnp.where(last, zero, tracer[lat])
        cx = {lat: courant(field(0, lat)) for lat in range(-1, 5)}
        cy = {lat: courant(field(1, lat)) for lat in range(-1, 5)}
        mine, upper, lower = edges[0, level, :], edges[1, level, :], edges[2, level, :]

        def side(f):
            return jnp.where(
                lane < 16,
                shift(upper, -(f * 32 + 16)),
                jnp.where(lane < 48, shift(mine, 16 - f * 32), shift(lower, 48 - f * 32)),
            )

        edge = side(2)
        edge = jnp.where(((lane < 16) & first) | ((lane >= 48) & last), zero, edge)
        edge_x, edge_y = courant(side(0)), courant(side(1))

        def beside(value, rim, lat):
            west = shift(value, 1)
            west = jnp.where(lane == 0, shift(rim, -((lat + 2) * 8 + 1)), west)
            east = shift(value, -1)
            east = jnp.where(lane == 127, shift(rim, 127 - ((lat + 2) * 8 + 4)), east)
            return west, east

        once = {}
        for lat in range(-1, 5):
            west, east = beside(tracer[lat], edge, lat)
            once[lat] = upwind(
                tracer[lat], west, east, tracer[lat - 1], tracer[lat + 1], cx[lat], cy[lat]
            )
        once[-1] = jnp.where(first, zero, once[-1])
        once[4] = jnp.where(last, zero, once[4])
        rim = upwind(
            edge, shift(edge, 1), shift(edge, -1), shift(edge, 8), shift(edge, -8), edge_x, edge_y
        )
        for lat in range(4):
            west, east = beside(once[lat], rim, lat)
            row = pl.ds(step * 32 + lat, 8, stride=4)
            out[row, :] = once[lat]
            change[row, :] = (
                jnp.maximum(cx[lat], 0.0) * (once[lat] - west)
                + jnp.minimum(cx[lat], 0.0) * (east - once[lat])
                + jnp.maximum(cy[lat], 0.0) * (once[lat] - once[lat - 1])
                + jnp.minimum(cy[lat], 0.0) * (once[lat + 1] - once[lat])
            )
        return carry

    lax.fori_loop(0, LEVS // 8, line, 0, unroll=2)


def all_in_one(
    numbers_far, line_far, spec_far, leg_far, order_far, table_far, edges_far, vertical_far, spread_far,
    out, change,
    numbers, line, spec, leg, order, table, edges, vertical, spread,
    load, leg_load,
    wide, turned, tall, gather, main, rest,
    main_in, choice, small, joined, part, grid, edge, message,
    own, north, south, modes, fields, rims,
    send, recv, here, block_recv, halo_send, halo_recv,
):
    w, v = lax.axis_index("wave"), lax.axis_index("lev")
    loads = [
        pltpu.make_async_copy(far, near, load.at[i])
        for i, (far, near) in enumerate(
            (
                (numbers_far, numbers),
                (spec_far, spec),
                (line_far, line),
                (order_far, order),
                (table_far, table),
                (edges_far, edges),
                (vertical_far, vertical),
                (spread_far, spread),
            )
        )
    ]

    def leg_copy(i):
        rows = pl.ds(4 * i, 4)
        return pltpu.make_async_copy(leg_far.at[rows], leg.at[rows], leg_load.at[i])

    for copy in loads[:2]:
        copy.start()
    for i in range(4):
        leg_copy(i).start()
    for copy in loads[2:]:
        copy.start()

    barrier = pltpu.get_barrier_semaphore()

    def greet(axis, count, own_index):
        def step(i, carry):
            other = lax.rem(own_index + i, count)
            pl.semaphore_signal(barrier, inc=1, device_id={axis: other}, device_id_type=MESH)
            return carry

        lax.fori_loop(1, count, step, 0)

    greet("wave", WAVES, w)
    greet("lev", LEVDEV, v)
    loads[0].wait()
    loads[1].wait()
    first = w * SLOTS
    legendre_stage(
        lambda s: numbers[first + s],
        spec, leg, lambda i: leg_copy(i).wait(), main, rest, wide, turned, tall, gather,
    )
    pl.semaphore_wait(barrier, WAVES + LEVDEV - 2)

    x, z = w // 8, lax.rem(w, 8)
    xs = [jnp.where(x + d >= 8, x + d - 8, x + d) * 8 for d in range(8)]
    zs = [jnp.where(z + d >= 8, z + d - 8, z + d) for d in range(8)]
    steps = [(dx, dz) for dx in range(8) for dz in range(8) if dx + dz > 0]
    steps.sort(key=lambda step: -sum(min(d, 8 - d) for d in step))

    def band_copy(src, dst, target):
        return pltpu.make_async_remote_copy(
            src_ref=src,
            dst_ref=dst,
            send_sem=send.at[0],
            recv_sem=recv.at[0],
            device_id={"wave": target},
            device_id_type=MESH,
        )

    for dx, dz in steps:
        target = xs[dx] + zs[dz]
        band_copy(main.at[target], main_in.at[w], target).start()
    local = pltpu.make_async_copy(main.at[w], main_in.at[w], here.at[0])
    local.start()
    for copy in loads[2:]:
        copy.wait()
    choose_rows(line[...], choice)
    top = vertical[...].astype(BF)
    low = (vertical[...] - top.astype(F32)).astype(BF)
    both = jnp.concatenate([top, low], axis=0)
    spread_both = dot(both, spread[...]).astype(BF)
    local.wait()
    many = pl.ds(0, WAVES - 1)
    whole = band_copy(main.at[many], main_in.at[many], xs[1] + zs[0])
    whole.wait_send()
    whole.wait_recv()

    shifts = [8] + [8 + sign * k for k in range(1, 8) for sign in (-1, 1)]

    def other_block(shift):
        block = v + shift
        return jnp.where(block >= LEVDEV, block - LEVDEV, block)

    def block_copy(src, dst, shift):
        return pltpu.make_async_remote_copy(
            src_ref=message.at[other_block(shift)] if src is None else src,
            dst_ref=dst,
            send_sem=send.at[1],
            recv_sem=block_recv.at[v],
            device_id={"lev": other_block(shift)},
            device_id_type=MESH,
        )

    def ready(tile, count):
        rows = pl.ds(tile, count)
        for shift in shifts:
            block_copy(
                message.at[other_block(shift), rows], own.at[v, rows], shift
            ).start()

    fourier_stage(
        main_in, rest, choice, order, table, edges, message, small, joined, part, grid, edge, ready
    )
    itself = pltpu.make_async_copy(message.at[v], own.at[v], here.at[1])
    itself.start()
    itself.wait()

    def halo_copy(i, src, dst):
        return pltpu.make_async_remote_copy(
            src_ref=src,
            dst_ref=dst,
            send_sem=halo_send.at[i],
            recv_sem=halo_recv.at[i],
            device_id={"wave": lax.rem(w + (1 if i == 0 else WAVES - 1), WAVES)},
            device_id_type=MESH,
        )

    def pass_on(block):
        halo_copy(0, own.at[block, pl.ds(6, 4)], north.at[block]).start()
        halo_copy(1, own.at[block, pl.ds(3, 4)], south.at[block]).start()
        row = pl.ds(pl.multiple_of(block * 24, 8), 24)
        for i, tile in enumerate((0, 3, 7)):
            modes[i, row, :] = own[block, tile : tile + 3].astype(F32).reshape(24, 128)

    pass_on(v)
    for shift in shifts:
        block = other_block(LEVDEV - shift)
        pltpu.make_async_remote_copy(
            src_ref=message.at[block],
            dst_ref=own.at[block],
            send_sem=send.at[1],
            recv_sem=block_recv.at[block],
            device_id={"lev": block},
            device_id_type=MESH,
        ).wait_recv()
        pass_on(block)
    modes_to_levels((0, 1, 2), both, modes, fields)
    rims_of(((0, own, EDGE_TILE),), spread_both, rims)
    many = pl.ds(0, LEVDEV - 1)
    block_copy(message.at[many], own.at[many], 1).wait_send()
    halo_copy(0, own.at[:, pl.ds(6, 4)], north).wait()
    halo_copy(1, own.at[:, pl.ds(3, 4)], south).wait()
    for i, ref, tile in ((3, north, 1), (4, south, 0)):
        for d in range(LEVDEV):
            modes[i, d * 24 : (d + 1) * 24, :] = ref[d, tile : tile + 3].astype(F32).reshape(24, 128)
    modes_to_levels((3, 4), both, modes, fields)
    rims_of(((1, north, 0), (2, south, 3)), spread_both, rims)
    upwind_stage(w, fields, rims, out, change)


def body(spectrum, legendre, wave_numbers, vertical):
    spec = jnp.transpose(spectrum, (2, 3, 0, 1)).reshape(COLS, SLOTS, NM)
    dma = pltpu.SemaphoreType.DMA
    far = pl.BlockSpec(memory_space=pl.ANY)
    near = pltpu.VMEM
    here = pl.BlockSpec(memory_space=pltpu.VMEM)
    message = (LEVDEV, 10, 8, 128)
    halo = (LEVDEV, 4, 8, 128)
    before, change = pl.pallas_call(
        all_in_one,
        name="synthesis",
        out_shape=(jax.ShapeDtypeStruct((LEVS * 4, 128), F32),) * 2,
        in_specs=[far] * 9,
        out_specs=(here, here),
        scratch_shapes=[
            pltpu.SMEM((NM,), jnp.int32),
            near((1, NM), jnp.int32),
            near((COLS, SLOTS, NM), BF),
            near((SLOTS, NM, 128), BF),
            near((144, 256), BF),
            near((RADIX, 256, 2 * SPAN), BF),
            near((NLON, 128), BF),
            near((LEVS, LEVS), F32),
            near((LEVS, 128), BF),
            dma((8,)),
            dma((4,)),
            near((8, 640, 128), F32),
            near((2, 4, 128, 128), F32),
            near((2, 256, 128), F32),
            near((WAVES * SLOTS, 128), F32),
            near((WAVES, 3, 8, 128), BF),
            near((WAVES * 8, 128), F32),
            near((WAVES, 3, 8, 128), BF),
            near((NM, NM), BF),
            near((NM, 128), F32),
            near((NM, 256), BF),
            near((RADIX, 72, 2 * SPAN), F32),
            near((72, NLON), F32),
            near((80, 128), F32),
            near(message, BF),
            near(message, BF),
            near(halo, BF),
            near(halo, BF),
            near((5, LEVDEV * 24, 128), F32),
            near((5, 4, LEVS, 128), F32),
            near((3, LEVS, 128), F32),
            dma((2,)),
            dma((1,)),
            dma((2,)),
            dma((LEVDEV,)),
            dma((2,)),
            dma((2,)),
        ],
        compiler_params=pltpu.CompilerParams(
            vmem_limit_bytes=60 * 2**20, collective_id=0, has_side_effects=True
        ),
    )(
        wave_numbers,
        wave_numbers.reshape(1, NM),
        spec,
        legendre,
        jnp.asarray(row_table()),
        jnp.asarray(fourier_table()),
        jnp.asarray(edge_table()),
        vertical,
        jnp.asarray(spread_table()),
    )
    return (before - change).reshape(LEVS, 4, 128)


def solution(mesh):
    placed = (P("wave", None, "lev", None), P("wave", None, None), P(), P())
    return jax.shard_map(
        body, mesh=mesh, in_specs=placed, out_specs=P(None, "wave", "lev"), check_vma=False
    )
```

```python
import jax
import jax.numpy as jnp
import numpy as np
from jax import lax
from jax.experimental import pallas as pl
from jax.experimental.pallas import tpu as pltpu
from jax.sharding import PartitionSpec as P

BF = jnp.bfloat16
F32 = jnp.float32
MESH = pl.DeviceIdType.MESH
COURANT = 0.45

NM = 1024
NLON = 2048
LEVS = 96
WAVES = 64
LEVDEV = 16
SLOTS = 16
COLS = 36
MODES = 6
RADIX = 8
SPAN = NLON // RADIX

GROUPS = (
    ((0, 1), (1, 1), (0, 2), (1, 2)),
    ((0, 0), (1, 0), (2, 0), (2, 1)),
    ((2, 2), (2, 3), (1, 3), (0, 3)),
)
PLACE = {pair: (g, i) for g, group in enumerate(GROUPS) for i, pair in enumerate(group)}
EDGE_TILE = 6
OFFSETS = (-2, -1, 0, 127, 128, 129)


def fourier_table():
    numbers = np.arange(NM).reshape(NM // RADIX, RADIX).T
    residue = numbers[:, :, None] * np.arange(SPAN)[None, None, :] % NLON
    angle = residue * (2.0 * np.pi / NLON)
    weight = np.where(numbers == 0, 1.0, 2.0)[:, :, None]
    real, imaginary = weight * np.cos(angle), weight * np.sin(angle)
    imaginary = np.where(residue == 0, 0.0, imaginary)
    top = np.concatenate([real, imaginary], axis=2)
    bottom = np.concatenate([-imaginary, real], axis=2)
    return np.concatenate([top, bottom], axis=1).astype(BF)


def row_table():
    table = np.zeros((144, 256), np.float32)
    for (field, lat), (group, place) in PLACE.items():
        for mode in range(MODES):
            for part in range(2):
                pair = mode * 3 + field
                if pair < 16:
                    column = part * 64 + lat * 16 + pair
                else:
                    column = 128 + lat * 4 + (pair - 16) * 2 + part
                table[part * 72 + group * 24 + mode * 4 + place, column] = 1.0
    return table.astype(BF)


def edge_table():
    numbers = np.arange(NM).reshape(NM // RADIX, RADIX).T
    residue = np.zeros((RADIX, NM // RADIX, 128), np.int64)
    used = np.zeros(128)
    for block in range(LEVDEV):
        for k, offset in enumerate(OFFSETS):
            residue[:, :, block * 8 + k] = numbers * ((block * 128 + offset) % NLON) % NLON
            used[block * 8 + k] = 1.0
    angle = residue * (2.0 * np.pi / NLON)
    weight = np.where(numbers == 0, 1.0, 2.0)[:, :, None] * used
    imaginary = np.where(residue % (NLON // 2) == 0, 0.0, weight * np.sin(angle))
    return np.concatenate([weight * np.cos(angle), -imaginary], axis=1).astype(BF)


def spread_table():
    table = np.zeros((LEVS, 128), np.float32)
    for mode in range(LEVS):
        table[mode, mode // MODES * 8 + mode % MODES] = 1.0
    return table.astype(BF)


def dot(a, b):
    return jnp.dot(a, b, preferred_element_type=F32)


def pick(values, index):
    result = values[-1]
    for i in range(len(values) - 2, -1, -1):
        result = jnp.where(index == i, values[i], result)
    return result


def legendre_stage(numbers, spec, leg, arrived, main, rest, wide, turned, tall, gather):
    rest[...] = jnp.zeros_like(rest)
    for c in range(COLS + 4):
        values = spec[c if c < COLS else c - 4].astype(F32)
        for k in range(8):
            wide[k, c * SLOTS : (c + 1) * SLOTS, :] = values[:, k * 128 : (k + 1) * 128]
    degree = lax.broadcasted_iota(jnp.int32, (1, NM), 1)
    sign = jnp.where(degree % 2 == 1, -1.0, 1.0)
    lane = lax.broadcasted_iota(jnp.int32, (32, 128), 1)
    turn = lane // 16 % 4
    small = lane // 4 % 4

    def slot(s, j):
        rows = jnp.concatenate(
            [
                jnp.concatenate(
                    [
                        wide[k, pl.ds(s, 16, stride=32), :],
                        wide[k, pl.ds(16 + s, 16, stride=32), :],
                        wide[k, pl.ds(512 + s, 8, stride=16), :],
                    ],
                    axis=0,
                )
                for k in range(8)
            ],
            axis=1,
        )
        counted = jnp.where(degree < NM - numbers(s), 1.0, 0.0)
        both = jnp.concatenate([rows * counted, rows * (counted * sign)], axis=0).astype(BF)
        sums = dot(both, leg[s])
        for half in range(2):
            own = sums[half * 40 : (half + 1) * 40]
            block = jnp.concatenate([own[0:16]] * 4 + [own[16:32]] * 4, axis=0)
            turned[half, j] = block.T
            lines = [turned[half, j, pl.ds(r, 32, stride=4), :] for r in range(4)]
            if half == 1:
                lines = lines[::-1]
            gather[pl.ds(half * 512 + s, 32, stride=SLOTS), :] = pick(lines, turn)
            tall[half, pl.ds(pl.multiple_of(s * 16, 16), 16), :] = jnp.concatenate(
                [own[32:40]] * 2, axis=0
            )

    def group(i, carry):
        arrived(i)
        for j in range(4):
            slot(4 * i + j, j)
        return carry

    lax.fori_loop(0, 4, group, 0)
    for half in range(2):
        for h in range(2):
            turned[half, h] = tall[half, h * 128 : (h + 1) * 128, :].T
            lines = [turned[half, h, pl.ds(r, 32, stride=4), :] for r in range(4)]
            if half == 1:
                lines = lines[::-1]
            rest[pl.ds(half * 256 + h, 32, stride=8), :] = pick(lines, small)
    for b in range(WAVES):
        band = b if b < 32 else 95 - b
        main[band, 0:2] = gather[b * SLOTS : (b + 1) * SLOTS, :].astype(BF).reshape(2, 8, 128)
        main[band, 2] = rest[b * 8 : (b + 1) * 8, :].astype(BF)


def choose_rows(numbers, choice):
    line = lax.broadcasted_iota(jnp.int32, (32, NM), 0)

    def step(i, carry):
        wanted = i // 4 + RADIX * (i % 4 * 32 + line)
        hit = jnp.where(numbers == wanted, 1.0, 0.0).astype(BF)
        choice[pl.ds(pl.multiple_of(i * 32, 32), 32), :] = hit
        return carry

    lax.fori_loop(0, 32, step, 0)


def fourier_stage(main, rest, choice, order, table, edges, message, small, joined, part, edge, ready):
    joined[:, 0:128] = main[:, 0:2].reshape(NM, 128)
    for i in range(8):
        tiles = main[i * 8 : (i + 1) * 8, 2].astype(F32)
        rest[i * 64 : (i + 1) * 64, :] = tiles.reshape(64, 128)
    for h in range(2):
        values = rest[pl.ds(h, WAVES, stride=8), :]
        for g in range(8):
            rolled = values if g == 0 else pltpu.roll(values, 128 - 16 * g, 1)
            small[pl.ds(h * 8 + g, WAVES, stride=SLOTS), :] = rolled
    joined[:, 128:256] = small[...].astype(BF)
    ordered = dot(choice[...], joined[...]).astype(BF)
    lines = lax.dot_general(
        order[...], ordered, (((1,), (1,)), ((), ())), preferred_element_type=F32
    )
    for k in range(RADIX):
        own = lines[:, k * 128 : (k + 1) * 128]
        pair = jnp.concatenate([own[0:72].astype(BF), own[72:144].astype(BF)], axis=1)
        part[k] = dot(pair, table[k])
        rim = dot(pair, edges[k])
        total = rim if k == 0 else total + rim
    edge[0:72] = total
    edge[72:80] = jnp.zeros((8, 128), F32)
    root = 0.5**0.5

    def combine(i, carry):
        row = pl.ds(pl.multiple_of(i * 8, 8), 8)
        tile = i + jnp.where(i >= EDGE_TILE, 1, 0)
        for h in range(2):
            re = [part[k, row, h * 128 : (h + 1) * 128] for k in range(RADIX)]
            im = [
                None if k % 4 == 0 else part[k, row, SPAN + h * 128 : SPAN + (h + 1) * 128]
                for k in range(RADIX)
            ]
            plus, minus = re[0] + re[4], re[0] - re[4]
            level, cross = re[2] + re[6], im[6] - im[2]
            even = [plus + level, minus + cross, plus - level, minus - cross]
            a, b = re[1] - re[5], re[7] - re[3]
            c, d = im[5] - im[1], im[7] - im[3]
            odd = [
                re[1] + re[3] + re[5] + re[7],
                root * (a + b + c + d),
                im[3] - im[1] + im[7] - im[5],
                root * (c + d - a - b),
            ]
            for u in range(RADIX):
                value = even[u % 4] + odd[u] if u < 4 else even[u % 4] - odd[u - 4]
                message[2 * u + h, tile] = value.astype(BF)
        return carry

    lane = lax.broadcasted_iota(jnp.int32, (8, 128), 1) // 8

    def pack(block, carry):
        total = jnp.zeros((8, 128), F32)
        for field in range(3):
            for lat in range(4):
                group, place = PLACE[(field, lat)]
                q = field * 4 + lat
                values = edge[pl.ds(group * 24 + place, 8, stride=4), :]
                rolled = pltpu.roll(values, (128 + 8 * q - 8 * block) % 128, 1)
                total = jnp.where(lane == q, rolled, total)
        message[block, EDGE_TILE] = total.astype(BF)
        return carry

    lax.fori_loop(0, LEVDEV, pack, 0)
    lax.fori_loop(3, 6, combine, 0)
    ready(3, 4, 0)
    lax.fori_loop(6, 9, combine, 0)
    ready(7, 3, 0)
    lax.fori_loop(0, 3, combine, 0)
    ready(0, 3, 1)


def modes_to_levels(groups, both, wide, fields):
    for i in groups:
        for q in range(0, 4, 2):
            modes = jnp.concatenate(
                [wide[i, pl.ds(q, LEVS, stride=4), :], wide[i, pl.ds(q + 1, LEVS, stride=4), :]],
                axis=1,
            ).astype(BF)
            twice = dot(both, modes)
            value = twice[:LEVS] + twice[LEVS:]
            fields[i, q] = value[:, :128]
            fields[i, q + 1] = value[:, 128:]


def rims_of(sources, spread_both, rims):
    for i, ref, tile in sources:
        twice = dot(spread_both, ref[:, tile].reshape(128, 128))
        rims[i] = twice[:LEVS] + twice[LEVS:]


def upwind_stage(band, fields, edges, out, change):
    lane = lax.broadcasted_iota(jnp.int32, (8, 128), 1)
    first, last = band == 0, band == WAVES - 1

    def where_is(field, lat):
        if lat < 0:
            group, place = PLACE[(field, lat + 4)]
            return 3, place
        if lat > 3:
            group, place = PLACE[(field, lat - 4)]
            return 4, place
        return PLACE[(field, lat)]

    def shift(value, amount):
        amount = amount % 128
        return value if amount == 0 else pltpu.roll(value, amount, 1)

    def upwind(center, west, east, north, south, cx, cy):
        return (
            center
            - jnp.maximum(cx, 0.0) * (center - west)
            - jnp.minimum(cx, 0.0) * (east - center)
            - jnp.maximum(cy, 0.0) * (center - north)
            - jnp.minimum(cy, 0.0) * (south - center)
        )

    def line(step, carry):
        level = pl.ds(pl.multiple_of(step * 8, 8), 8)

        def field(f, lat):
            i, q = where_is(f, lat)
            return fields[i, q, level, :]

        def courant(value):
            return COURANT * jnp.tanh(value)

        zero = jnp.zeros((8, 128), F32)
        tracer = {lat: field(2, lat) for lat in range(-2, 6)}
        for lat in (-2, -1):
            tracer[lat] = jnp.where(first, zero, tracer[lat])
        for lat in (4, 5):
            tracer[lat] = jnp.where(last, zero, tracer[lat])
        cx = {lat: courant(field(0, lat)) for lat in range(-1, 5)}
        cy = {lat: courant(field(1, lat)) for lat in range(-1, 5)}
        mine, upper, lower = edges[0, level, :], edges[1, level, :], edges[2, level, :]

        def side(f):
            return jnp.where(
                lane < 16,
                shift(upper, -(f * 32 + 16)),
                jnp.where(lane < 48, shift(mine, 16 - f * 32), shift(lower, 48 - f * 32)),
            )

        edge = side(2)
        edge = jnp.where(((lane < 16) & first) | ((lane >= 48) & last), zero, edge)
        edge_x, edge_y = courant(side(0)), courant(side(1))

        def beside(value, rim, lat):
            west = shift(value, 1)
            west = jnp.where(lane == 0, shift(rim, -((lat + 2) * 8 + 1)), west)
            east = shift(value, -1)
            east = jnp.where(lane == 127, shift(rim, 127 - ((lat + 2) * 8 + 4)), east)
            return west, east

        once = {}
        for lat in range(-1, 5):
            west, east = beside(tracer[lat], edge, lat)
            once[lat] = upwind(
                tracer[lat], west, east, tracer[lat - 1], tracer[lat + 1], cx[lat], cy[lat]
            )
        once[-1] = jnp.where(first, zero, once[-1])
        once[4] = jnp.where(last, zero, once[4])
        rim = upwind(
            edge, shift(edge, 1), shift(edge, -1), shift(edge, 8), shift(edge, -8), edge_x, edge_y
        )
        for lat in range(4):
            west, east = beside(once[lat], rim, lat)
            row = pl.ds(step * 32 + lat, 8, stride=4)
            out[row, :] = once[lat]
            change[row, :] = (
                jnp.maximum(cx[lat], 0.0) * (once[lat] - west)
                + jnp.minimum(cx[lat], 0.0) * (east - once[lat])
                + jnp.maximum(cy[lat], 0.0) * (once[lat] - once[lat - 1])
                + jnp.minimum(cy[lat], 0.0) * (once[lat + 1] - once[lat])
            )
        return carry

    lax.fori_loop(0, LEVS // 8, line, 0, unroll=2)


def all_in_one(
    numbers_far, line_far, spec_far, leg_far, order_far, table_far, edges_far, vertical_far, spread_far,
    out, change,
    numbers, line, spec, leg, order, table, edges, vertical, spread,
    load, leg_load,
    wide, turned, tall, gather, main, rest,
    main_in, choice, small, joined, part, edge, message,
    own, north, south, modes, fields, rims,
    send, recv, here, block_recv, halo_send, halo_recv,
):
    w, v = lax.axis_index("wave"), lax.axis_index("lev")
    loads = [
        pltpu.make_async_copy(far, near, load.at[i])
        for i, (far, near) in enumerate(
            (
                (numbers_far, numbers),
                (spec_far, spec),
                (line_far, line),
                (order_far, order),
                (table_far, table),
                (edges_far, edges),
                (vertical_far, vertical),
                (spread_far, spread),
            )
        )
    ]

    def leg_copy(i):
        rows = pl.ds(4 * i, 4)
        return pltpu.make_async_copy(leg_far.at[rows], leg.at[rows], leg_load.at[i])

    for copy in loads[:2]:
        copy.start()
    for i in range(4):
        leg_copy(i).start()
    for copy in loads[2:]:
        copy.start()

    barrier = pltpu.get_barrier_semaphore()

    def greet(axis, count, own_index):
        def step(i, carry):
            other = lax.rem(own_index + i, count)
            pl.semaphore_signal(barrier, inc=1, device_id={axis: other}, device_id_type=MESH)
            return carry

        lax.fori_loop(1, count, step, 0)

    x, z = w // 8, lax.rem(w, 8)
    xs = [jnp.where(x + d >= 8, x + d - 8, x + d) * 8 for d in range(8)]
    zs = [jnp.where(z + d >= 8, z + d - 8, z + d) for d in range(8)]
    steps = [(dx, dz) for dx in range(8) for dz in range(8) if dx + dz > 0]
    steps.sort(key=lambda step: -sum(min(d, 8 - d) for d in step))
    for dx, dz in steps:
        target = xs[dx] + zs[dz]
        pl.semaphore_signal(barrier, inc=1, device_id={"wave": target}, device_id_type=MESH)
    greet("lev", LEVDEV, v)
    loads[0].wait()
    loads[1].wait()
    first = w * SLOTS
    legendre_stage(
        lambda s: numbers[first + s],
        spec, leg, lambda i: leg_copy(i).wait(), main, rest, wide, turned, tall, gather,
    )
    pl.semaphore_wait(barrier, WAVES + LEVDEV - 2)

    def band_copy(src, dst, target):
        return pltpu.make_async_remote_copy(
            src_ref=src,
            dst_ref=dst,
            send_sem=send.at[0],
            recv_sem=recv.at[0],
            device_id={"wave": target},
            device_id_type=MESH,
        )

    for dx, dz in steps:
        target = xs[dx] + zs[dz]
        band_copy(main.at[target], main_in.at[w], target).start()
    local = pltpu.make_async_copy(main.at[w], main_in.at[w], here.at[0])
    local.start()
    for copy in loads[2:]:
        copy.wait()
    choose_rows(line[...], choice)
    top = vertical[...].astype(BF)
    low = (vertical[...] - top.astype(F32)).astype(BF)
    both = jnp.concatenate([top, low], axis=0)
    spread_both = dot(both, spread[...]).astype(BF)
    local.wait()
    many = pl.ds(0, WAVES - 1)
    whole = band_copy(main.at[many], main_in.at[many], xs[1] + zs[0])
    whole.wait_send()
    whole.wait_recv()

    shifts = [8] + [8 + sign * k for k in range(1, 8) for sign in (-1, 1)]

    def other_block(shift):
        block = v + shift
        return jnp.where(block >= LEVDEV, block - LEVDEV, block)

    def block_copy(src, dst, shift, kind):
        return pltpu.make_async_remote_copy(
            src_ref=src,
            dst_ref=dst,
            send_sem=send.at[1 + kind],
            recv_sem=block_recv.at[kind, v],
            device_id={"lev": other_block(shift)},
            device_id_type=MESH,
        )

    def ready(tile, count, kind):
        rows = pl.ds(tile, count)
        for shift in shifts:
            block_copy(
                message.at[other_block(shift), rows], own.at[v, rows], shift, kind
            ).start()

    fourier_stage(
        main_in, rest, choice, order, table, edges, message, small, joined, part, edge, ready
    )
    itself = pltpu.make_async_copy(message.at[v], own.at[v], here.at[1])
    itself.start()
    itself.wait()

    def halo_copy(i, src, dst):
        return pltpu.make_async_remote_copy(
            src_ref=src,
            dst_ref=dst,
            send_sem=halo_send.at[i],
            recv_sem=halo_recv.at[i],
            device_id={"wave": lax.rem(w + (1 if i == 0 else WAVES - 1), WAVES)},
            device_id_type=MESH,
        )

    def pass_on(block):
        halo_copy(0, own.at[block, pl.ds(6, 4)], north.at[block]).start()
        halo_copy(1, own.at[block, pl.ds(3, 4)], south.at[block]).start()
        widen(block, ((1, 3), (2, 7)))

    def widen(block, pairs):
        row = pl.ds(pl.multiple_of(block * 24, 8), 24)
        for i, tile in pairs:
            modes[i, row, :] = own[block, tile : tile + 3].astype(F32).reshape(24, 128)

    def arrived(block, rows, kind):
        pltpu.make_async_remote_copy(
            src_ref=message.at[block, rows],
            dst_ref=own.at[block, rows],
            send_sem=send.at[1 + kind],
            recv_sem=block_recv.at[kind, block],
            device_id={"lev": block},
            device_id_type=MESH,
        ).wait_recv()

    pass_on(v)
    for shift in shifts:
        block = other_block(LEVDEV - shift)
        arrived(block, pl.ds(3, 7), 0)
        pass_on(block)
    widen(v, ((0, 0),))
    for shift in shifts:
        block = other_block(LEVDEV - shift)
        arrived(block, pl.ds(0, 3), 1)
        widen(block, ((0, 0),))
    modes_to_levels((0, 1, 2), both, modes, fields)
    rims_of(((0, own, EDGE_TILE),), spread_both, rims)
    many = pl.ds(0, LEVDEV - 1)
    for kind, rows in enumerate((pl.ds(3, 7), pl.ds(0, 3))):
        block_copy(message.at[many, rows], own.at[many, rows], 1, kind).wait_send()
    halo_copy(0, own.at[:, pl.ds(6, 4)], north).wait()
    halo_copy(1, own.at[:, pl.ds(3, 4)], south).wait()
    for i, ref, tile in ((3, north, 1), (4, south, 0)):
        for d in range(LEVDEV):
            modes[i, d * 24 : (d + 1) * 24, :] = ref[d, tile : tile + 3].astype(F32).reshape(24, 128)
    modes_to_levels((3, 4), both, modes, fields)
    rims_of(((1, north, 0), (2, south, 3)), spread_both, rims)
    upwind_stage(w, fields, rims, out, change)


def body(spectrum, legendre, wave_numbers, vertical):
    spec = jnp.transpose(spectrum, (2, 3, 0, 1)).reshape(COLS, SLOTS, NM)
    dma = pltpu.SemaphoreType.DMA
    far = pl.BlockSpec(memory_space=pl.ANY)
    near = pltpu.VMEM
    here = pl.BlockSpec(memory_space=pltpu.VMEM)
    message = (LEVDEV, 10, 8, 128)
    halo = (LEVDEV, 4, 8, 128)
    before, change = pl.pallas_call(
        all_in_one,
        name="synthesis",
        out_shape=(jax.ShapeDtypeStruct((LEVS * 4, 128), F32),) * 2,
        in_specs=[far] * 9,
        out_specs=(here, here),
        scratch_shapes=[
            pltpu.SMEM((NM,), jnp.int32),
            near((1, NM), jnp.int32),
            near((COLS, SLOTS, NM), BF),
            near((SLOTS, NM, 128), BF),
            near((144, 256), BF),
            near((RADIX, 256, 2 * SPAN), BF),
            near((RADIX, 256, 128), BF),
            near((LEVS, LEVS), F32),
            near((LEVS, 128), BF),
            dma((8,)),
            dma((4,)),
            near((8, 640, 128), F32),
            near((2, 4, 128, 128), F32),
            near((2, 256, 128), F32),
            near((WAVES * SLOTS, 128), F32),
            near((WAVES, 3, 8, 128), BF),
            near((WAVES * 8, 128), F32),
            near((WAVES, 3, 8, 128), BF),
            near((NM, NM), BF),
            near((NM, 128), F32),
            near((NM, 256), BF),
            near((RADIX, 72, 2 * SPAN), F32),
            near((80, 128), F32),
            near(message, BF),
            near(message, BF),
            near(halo, BF),
            near(halo, BF),
            near((5, LEVDEV * 24, 128), F32),
            near((5, 4, LEVS, 128), F32),
            near((3, LEVS, 128), F32),
            dma((3,)),
            dma((1,)),
            dma((2,)),
            dma((2, LEVDEV)),
            dma((2,)),
            dma((2,)),
        ],
        compiler_params=pltpu.CompilerParams(
            vmem_limit_bytes=60 * 2**20, collective_id=0, has_side_effects=True
        ),
    )(
        wave_numbers,
        wave_numbers.reshape(1, NM),
        spec,
        legendre,
        jnp.asarray(row_table()),
        jnp.asarray(fourier_table()),
        jnp.asarray(edge_table()),
        vertical,
        jnp.asarray(spread_table()),
    )
    return (before - change).reshape(LEVS, 4, 128)


def solution(mesh):
    placed = (P("wave", None, "lev", None), P("wave", None, None), P(), P())
    return jax.shard_map(
        body, mesh=mesh, in_specs=placed, out_specs=P(None, "wave", "lev"), check_vma=False
    )
```

```python
import jax
import jax.numpy as jnp
import numpy as np
from jax import lax
from jax.experimental import pallas as pl
from jax.experimental.pallas import tpu as pltpu
from jax.sharding import PartitionSpec as P

BF = jnp.bfloat16
F32 = jnp.float32
MESH = pl.DeviceIdType.MESH
COURANT = 0.45

NM = 1024
NLON = 2048
LEVS = 96
WAVES = 64
LEVDEV = 16
SLOTS = 16
COLS = 36
MODES = 6
RADIX = 8
SPAN = NLON // RADIX

GROUPS = (
    ((0, 1), (1, 1), (0, 2), (1, 2)),
    ((0, 0), (1, 0), (2, 0), (2, 1)),
    ((2, 2), (2, 3), (1, 3), (0, 3)),
)
PLACE = {pair: (g, i) for g, group in enumerate(GROUPS) for i, pair in enumerate(group)}
EDGE_TILE = 6
OFFSETS = (-2, -1, 0, 127, 128, 129)


def fourier_table():
    numbers = np.arange(NM).reshape(NM // RADIX, RADIX).T
    residue = numbers[:, :, None] * np.arange(SPAN)[None, None, :] % NLON
    angle = residue * (2.0 * np.pi / NLON)
    weight = np.where(numbers == 0, 1.0, 2.0)[:, :, None]
    real, imaginary = weight * np.cos(angle), weight * np.sin(angle)
    imaginary = np.where(residue == 0, 0.0, imaginary)
    top = np.concatenate([real, imaginary], axis=2)
    bottom = np.concatenate([-imaginary, real], axis=2)
    return np.concatenate([top, bottom], axis=1).astype(BF)


def row_table():
    table = np.zeros((144, 256), np.float32)
    for (field, lat), (group, place) in PLACE.items():
        for mode in range(MODES):
            for part in range(2):
                pair = mode * 3 + field
                if pair < 16:
                    column = part * 64 + lat * 16 + pair
                else:
                    column = 128 + lat * 4 + (pair - 16) * 2 + part
                table[part * 72 + group * 24 + mode * 4 + place, column] = 1.0
    return table.astype(BF)


def edge_table():
    numbers = np.arange(NM).reshape(NM // RADIX, RADIX).T
    residue = np.zeros((RADIX, NM // RADIX, 128), np.int64)
    used = np.zeros(128)
    for block in range(LEVDEV):
        for k, offset in enumerate(OFFSETS):
            residue[:, :, block * 8 + k] = numbers * ((block * 128 + offset) % NLON) % NLON
            used[block * 8 + k] = 1.0
    angle = residue * (2.0 * np.pi / NLON)
    weight = np.where(numbers == 0, 1.0, 2.0)[:, :, None] * used
    imaginary = np.where(residue % (NLON // 2) == 0, 0.0, weight * np.sin(angle))
    return np.concatenate([weight * np.cos(angle), -imaginary], axis=1).astype(BF)


def spread_table():
    table = np.zeros((LEVS, 128), np.float32)
    for mode in range(LEVS):
        table[mode, mode // MODES * 8 + mode % MODES] = 1.0
    return table.astype(BF)


def dot(a, b):
    return jnp.dot(a, b, preferred_element_type=F32)


def pick(values, index):
    result = values[-1]
    for i in range(len(values) - 2, -1, -1):
        result = jnp.where(index == i, values[i], result)
    return result


def legendre_stage(numbers, spec, leg, arrived, main, rest, wide, turned, tall, gather):
    rest[...] = jnp.zeros_like(rest)
    for c in range(COLS + 4):
        values = spec[c if c < COLS else c - 4].astype(F32)
        for k in range(8):
            wide[k, c * SLOTS : (c + 1) * SLOTS, :] = values[:, k * 128 : (k + 1) * 128]
    degree = lax.broadcasted_iota(jnp.int32, (1, NM), 1)
    sign = jnp.where(degree % 2 == 1, -1.0, 1.0)
    lane = lax.broadcasted_iota(jnp.int32, (32, 128), 1)
    turn = lane // 16 % 4
    small = lane // 4 % 4

    def slot(s, j):
        rows = jnp.concatenate(
            [
                jnp.concatenate(
                    [
                        wide[k, pl.ds(s, 16, stride=32), :],
                        wide[k, pl.ds(16 + s, 16, stride=32), :],
                        wide[k, pl.ds(512 + s, 8, stride=16), :],
                    ],
                    axis=0,
                )
                for k in range(8)
            ],
            axis=1,
        )
        counted = jnp.where(degree < NM - numbers(s), 1.0, 0.0)
        both = jnp.concatenate([rows * counted, rows * (counted * sign)], axis=0).astype(BF)
        sums = dot(both, leg[s])
        for half in range(2):
            own = sums[half * 40 : (half + 1) * 40]
            block = jnp.concatenate([own[0:16]] * 4 + [own[16:32]] * 4, axis=0)
            turned[half, j] = block.T
            lines = [turned[half, j, pl.ds(r, 32, stride=4), :] for r in range(4)]
            if half == 1:
                lines = lines[::-1]
            gather[pl.ds(half * 512 + s, 32, stride=SLOTS), :] = pick(lines, turn)
            tall[half, pl.ds(pl.multiple_of(s * 16, 16), 16), :] = jnp.concatenate(
                [own[32:40]] * 2, axis=0
            )

    def group(i, carry):
        arrived(i)
        for j in range(4):
            slot(4 * i + j, j)
        return carry

    lax.fori_loop(0, 4, group, 0)
    for half in range(2):
        for h in range(2):
            turned[half, h] = tall[half, h * 128 : (h + 1) * 128, :].T
            lines = [turned[half, h, pl.ds(r, 32, stride=4), :] for r in range(4)]
            if half == 1:
                lines = lines[::-1]
            rest[pl.ds(half * 256 + h, 32, stride=8), :] = pick(lines, small)
    for b in range(WAVES):
        band = b if b < 32 else 95 - b
        main[band, 0:2] = gather[b * SLOTS : (b + 1) * SLOTS, :].astype(BF).reshape(2, 8, 128)
        main[band, 2] = rest[b * 8 : (b + 1) * 8, :].astype(BF)


def choose_rows(numbers, choice):
    line = lax.broadcasted_iota(jnp.int32, (32, NM), 0)

    def step(i, carry):
        wanted = i // 4 + RADIX * (i % 4 * 32 + line)
        hit = jnp.where(numbers == wanted, 1.0, 0.0).astype(BF)
        choice[pl.ds(pl.multiple_of(i * 32, 32), 32), :] = hit
        return carry

    lax.fori_loop(0, 32, step, 0)


def fourier_stage(main, rest, choice, order, table, edges, message, small, joined, part, edge, ready):
    joined[:, 0:128] = main[:, 0:2].reshape(NM, 128)
    for i in range(8):
        tiles = main[i * 8 : (i + 1) * 8, 2].astype(F32)
        rest[i * 64 : (i + 1) * 64, :] = tiles.reshape(64, 128)
    for h in range(2):
        values = rest[pl.ds(h, WAVES, stride=8), :]
        for g in range(8):
            rolled = values if g == 0 else pltpu.roll(values, 128 - 16 * g, 1)
            small[pl.ds(h * 8 + g, WAVES, stride=SLOTS), :] = rolled
    joined[:, 128:256] = small[...].astype(BF)
    ordered = dot(choice[...], joined[...]).astype(BF)
    lines = lax.dot_general(
        order[...], ordered, (((1,), (1,)), ((), ())), preferred_element_type=F32
    )
    for k in range(RADIX):
        own = lines[:, k * 128 : (k + 1) * 128]
        pair = jnp.concatenate([own[0:72].astype(BF), own[72:144].astype(BF)], axis=1)
        part[k] = dot(pair, table[k])
        rim = dot(pair, edges[k])
        total = rim if k == 0 else total + rim
    edge[0:72] = total
    edge[72:80] = jnp.zeros((8, 128), F32)
    root = 0.5**0.5

    def combine(i, carry):
        row = pl.ds(pl.multiple_of(i * 8, 8), 8)
        tile = i + jnp.where(i >= EDGE_TILE, 1, 0)
        for h in range(2):
            re = [part[k, row, h * 128 : (h + 1) * 128] for k in range(RADIX)]
            im = [
                None if k % 4 == 0 else part[k, row, SPAN + h * 128 : SPAN + (h + 1) * 128]
                for k in range(RADIX)
            ]
            plus, minus = re[0] + re[4], re[0] - re[4]
            level, cross = re[2] + re[6], im[6] - im[2]
            even = [plus + level, minus + cross, plus - level, minus - cross]
            a, b = re[1] - re[5], re[7] - re[3]
            c, d = im[5] - im[1], im[7] - im[3]
            odd = [
                re[1] + re[3] + re[5] + re[7],
                root * (a + b + c + d),
                im[3] - im[1] + im[7] - im[5],
                root * (c + d - a - b),
            ]
            for u in range(RADIX):
                value = even[u % 4] + odd[u] if u < 4 else even[u % 4] - odd[u - 4]
                message[2 * u + h, tile] = value.astype(BF)
        return carry

    lane = lax.broadcasted_iota(jnp.int32, (8, 128), 1) // 8

    def pack(block, carry):
        total = jnp.zeros((8, 128), F32)
        for field in range(3):
            for lat in range(4):
                group, place = PLACE[(field, lat)]
                q = field * 4 + lat
                values = edge[pl.ds(group * 24 + place, 8, stride=4), :]
                rolled = pltpu.roll(values, (128 + 8 * q - 8 * block) % 128, 1)
                total = jnp.where(lane == q, rolled, total)
        message[block, EDGE_TILE] = total.astype(BF)
        return carry

    lax.fori_loop(0, 3, combine, 0)
    ready(0, 3)
    lax.fori_loop(3, 6, combine, 0)
    ready(3, 3)
    lax.fori_loop(0, LEVDEV, pack, 0)
    lax.fori_loop(6, 9, combine, 0)
    ready(6, 4)


def modes_to_levels(groups, both, wide, fields):
    for i in groups:
        for q in range(0, 4, 2):
            modes = jnp.concatenate(
                [wide[i, pl.ds(q, LEVS, stride=4), :], wide[i, pl.ds(q + 1, LEVS, stride=4), :]],
                axis=1,
            ).astype(BF)
            twice = dot(both, modes)
            value = twice[:LEVS] + twice[LEVS:]
            fields[i, q] = value[:, :128]
            fields[i, q + 1] = value[:, 128:]


def rims_of(sources, spread_both, rims):
    for i, ref, tile in sources:
        twice = dot(spread_both, ref[:, tile].reshape(128, 128))
        rims[i] = twice[:LEVS] + twice[LEVS:]


def upwind_stage(band, fields, edges, out, change):
    lane = lax.broadcasted_iota(jnp.int32, (8, 128), 1)
    first, last = band == 0, band == WAVES - 1

    def where_is(field, lat):
        if lat < 0:
            group, place = PLACE[(field, lat + 4)]
            return 3, place
        if lat > 3:
            group, place = PLACE[(field, lat - 4)]
            return 4, place
        return PLACE[(field, lat)]

    def shift(value, amount):
        amount = amount % 128
        return value if amount == 0 else pltpu.roll(value, amount, 1)

    def upwind(center, west, east, north, south, cx, cy):
        return (
            center
            - jnp.maximum(cx, 0.0) * (center - west)
            - jnp.minimum(cx, 0.0) * (east - center)
            - jnp.maximum(cy, 0.0) * (center - north)
            - jnp.minimum(cy, 0.0) * (south - center)
        )

    def line(step, carry):
        level = pl.ds(pl.multiple_of(step * 8, 8), 8)

        def field(f, lat):
            i, q = where_is(f, lat)
            return fields[i, q, level, :]

        def courant(value):
            return COURANT * jnp.tanh(value)

        zero = jnp.zeros((8, 128), F32)
        tracer = {lat: field(2, lat) for lat in range(-2, 6)}
        for lat in (-2, -1):
            tracer[lat] = jnp.where(first, zero, tracer[lat])
        for lat in (4, 5):
            tracer[lat] = jnp.where(last, zero, tracer[lat])
        cx = {lat: courant(field(0, lat)) for lat in range(-1, 5)}
        cy = {lat: courant(field(1, lat)) for lat in range(-1, 5)}
        mine, upper, lower = edges[0, level, :], edges[1, level, :], edges[2, level, :]

        def side(f):
            return jnp.where(
                lane < 16,
                shift(upper, -(f * 32 + 16)),
                jnp.where(lane < 48, shift(mine, 16 - f * 32), shift(lower, 48 - f * 32)),
            )

        edge = side(2)
        edge = jnp.where(((lane < 16) & first) | ((lane >= 48) & last), zero, edge)
        edge_x, edge_y = courant(side(0)), courant(side(1))

        def beside(value, rim, lat):
            west = shift(value, 1)
            west = jnp.where(lane == 0, shift(rim, -((lat + 2) * 8 + 1)), west)
            east = shift(value, -1)
            east = jnp.where(lane == 127, shift(rim, 127 - ((lat + 2) * 8 + 4)), east)
            return west, east

        once = {}
        for lat in range(-1, 5):
            west, east = beside(tracer[lat], edge, lat)
            once[lat] = upwind(
                tracer[lat], west, east, tracer[lat - 1], tracer[lat + 1], cx[lat], cy[lat]
            )
        once[-1] = jnp.where(first, zero, once[-1])
        once[4] = jnp.where(last, zero, once[4])
        rim = upwind(
            edge, shift(edge, 1), shift(edge, -1), shift(edge, 8), shift(edge, -8), edge_x, edge_y
        )
        for lat in range(4):
            west, east = beside(once[lat], rim, lat)
            row = pl.ds(step * 32 + lat, 8, stride=4)
            out[row, :] = once[lat]
            change[row, :] = (
                jnp.maximum(cx[lat], 0.0) * (once[lat] - west)
                + jnp.minimum(cx[lat], 0.0) * (east - once[lat])
                + jnp.maximum(cy[lat], 0.0) * (once[lat] - once[lat - 1])
                + jnp.minimum(cy[lat], 0.0) * (once[lat + 1] - once[lat])
            )
        return carry

    lax.fori_loop(0, LEVS // 8, line, 0, unroll=2)


def all_in_one(
    numbers_far, line_far, spec_far, leg_far, order_far, table_far, edges_far, vertical_far, spread_far,
    out, change,
    numbers, line, spec, leg, order, table, edges, vertical, spread,
    load, leg_load,
    wide, turned, tall, gather, main, rest,
    main_in, choice, small, joined, part, edge, message,
    own, north, south, modes, fields, rims,
    send, recv, here, block_recv, halo_send, halo_recv,
):
    w, v = lax.axis_index("wave"), lax.axis_index("lev")
    loads = [
        pltpu.make_async_copy(far, near, load.at[i])
        for i, (far, near) in enumerate(
            (
                (numbers_far, numbers),
                (spec_far, spec),
                (line_far, line),
                (order_far, order),
                (table_far, table),
                (edges_far, edges),
                (vertical_far, vertical),
                (spread_far, spread),
            )
        )
    ]

    def leg_copy(i):
        rows = pl.ds(4 * i, 4)
        return pltpu.make_async_copy(leg_far.at[rows], leg.at[rows], leg_load.at[i])

    for copy in loads[:2]:
        copy.start()
    for i in range(4):
        leg_copy(i).start()
    for copy in loads[2:]:
        copy.start()

    barrier = pltpu.get_barrier_semaphore()

    def greet(axis, count, own_index):
        def step(i, carry):
            other = lax.rem(own_index + i, count)
            pl.semaphore_signal(barrier, inc=1, device_id={axis: other}, device_id_type=MESH)
            return carry

        lax.fori_loop(1, count, step, 0)

    x, z = w // 8, lax.rem(w, 8)
    xs = [jnp.where(x + d >= 8, x + d - 8, x + d) * 8 for d in range(8)]
    zs = [jnp.where(z + d >= 8, z + d - 8, z + d) for d in range(8)]
    steps = [(dx, dz) for dx in range(8) for dz in range(8) if dx + dz > 0]
    steps.sort(key=lambda step: -sum(min(d, 8 - d) for d in step))
    for dx, dz in steps:
        target = xs[dx] + zs[dz]
        pl.semaphore_signal(barrier, inc=1, device_id={"wave": target}, device_id_type=MESH)
    greet("lev", LEVDEV, v)
    loads[0].wait()
    loads[1].wait()
    first = w * SLOTS
    legendre_stage(
        lambda s: numbers[first + s],
        spec, leg, lambda i: leg_copy(i).wait(), main, rest, wide, turned, tall, gather,
    )
    pl.semaphore_wait(barrier, WAVES + LEVDEV - 2)

    def band_copy(src, dst, target):
        return pltpu.make_async_remote_copy(
            src_ref=src,
            dst_ref=dst,
            send_sem=send.at[0],
            recv_sem=recv.at[0],
            device_id={"wave": target},
            device_id_type=MESH,
        )

    for dx, dz in steps:
        target = xs[dx] + zs[dz]
        band_copy(main.at[target], main_in.at[w], target).start()
    local = pltpu.make_async_copy(main.at[w], main_in.at[w], here.at[0])
    local.start()
    for copy in loads[2:]:
        copy.wait()
    choose_rows(line[...], choice)
    top = vertical[...].astype(BF)
    low = (vertical[...] - top.astype(F32)).astype(BF)
    both = jnp.concatenate([top, low], axis=0)
    spread_both = dot(both, spread[...]).astype(BF)
    local.wait()
    many = pl.ds(0, WAVES - 1)
    whole = band_copy(main.at[many], main_in.at[many], xs[1] + zs[0])
    whole.wait_send()
    whole.wait_recv()

    shifts = [8] + [8 + sign * k for k in range(1, 8) for sign in (-1, 1)]

    def other_block(shift):
        block = v + shift
        return jnp.where(block >= LEVDEV, block - LEVDEV, block)

    def block_copy(src, dst, shift):
        return pltpu.make_async_remote_copy(
            src_ref=src,
            dst_ref=dst,
            send_sem=send.at[1],
            recv_sem=block_recv.at[v],
            device_id={"lev": other_block(shift)},
            device_id_type=MESH,
        )

    def ready(tile, count):
        rows = pl.ds(tile, count)
        for shift in shifts:
            block_copy(
                message.at[other_block(shift), rows], own.at[v, rows], shift
            ).start()

    fourier_stage(
        main_in, rest, choice, order, table, edges, message, small, joined, part, edge, ready
    )
    itself = pltpu.make_async_copy(message.at[v], own.at[v], here.at[1])
    itself.start()
    itself.wait()

    def halo_copy(i, src, dst):
        return pltpu.make_async_remote_copy(
            src_ref=src,
            dst_ref=dst,
            send_sem=halo_send.at[i],
            recv_sem=halo_recv.at[i],
            device_id={"wave": lax.rem(w + (1 if i == 0 else WAVES - 1), WAVES)},
            device_id_type=MESH,
        )

    def pass_on(block):
        halo_copy(0, own.at[block, pl.ds(6, 4)], north.at[block]).start()
        halo_copy(1, own.at[block, pl.ds(3, 4)], south.at[block]).start()
        row = pl.ds(pl.multiple_of(block * 24, 8), 24)
        for i, tile in enumerate((0, 3, 7)):
            modes[i, row, :] = own[block, tile : tile + 3].astype(F32).reshape(24, 128)

    pass_on(v)
    for shift in shifts:
        block = other_block(LEVDEV - shift)
        pltpu.make_async_remote_copy(
            src_ref=message.at[block],
            dst_ref=own.at[block],
            send_sem=send.at[1],
            recv_sem=block_recv.at[block],
            device_id={"lev": block},
            device_id_type=MESH,
        ).wait_recv()
        pass_on(block)
    modes_to_levels((0, 1, 2), both, modes, fields)
    rims_of(((0, own, EDGE_TILE),), spread_both, rims)
    many = pl.ds(0, LEVDEV - 1)
    block_copy(message.at[many], own.at[many], 1).wait_send()
    halo_copy(0, own.at[:, pl.ds(6, 4)], north).wait()
    halo_copy(1, own.at[:, pl.ds(3, 4)], south).wait()
    for i, ref, tile in ((3, north, 1), (4, south, 0)):
        for d in range(LEVDEV):
            modes[i, d * 24 : (d + 1) * 24, :] = ref[d, tile : tile + 3].astype(F32).reshape(24, 128)
    modes_to_levels((3, 4), both, modes, fields)
    rims_of(((1, north, 0), (2, south, 3)), spread_both, rims)
    upwind_stage(w, fields, rims, out, change)


def body(spectrum, legendre, wave_numbers, vertical):
    spec = jnp.transpose(spectrum, (2, 3, 0, 1)).reshape(COLS, SLOTS, NM)
    dma = pltpu.SemaphoreType.DMA
    far = pl.BlockSpec(memory_space=pl.ANY)
    near = pltpu.VMEM
    here = pl.BlockSpec(memory_space=pltpu.VMEM)
    message = (LEVDEV, 10, 8, 128)
    halo = (LEVDEV, 4, 8, 128)
    before, change = pl.pallas_call(
        all_in_one,
        name="synthesis",
        out_shape=(jax.ShapeDtypeStruct((LEVS * 4, 128), F32),) * 2,
        in_specs=[far] * 9,
        out_specs=(here, here),
        scratch_shapes=[
            pltpu.SMEM((NM,), jnp.int32),
            near((1, NM), jnp.int32),
            near((COLS, SLOTS, NM), BF),
            near((SLOTS, NM, 128), BF),
            near((144, 256), BF),
            near((RADIX, 256, 2 * SPAN), BF),
            near((RADIX, 256, 128), BF),
            near((LEVS, LEVS), F32),
            near((LEVS, 128), BF),
            dma((8,)),
            dma((4,)),
            near((8, 640, 128), F32),
            near((2, 4, 128, 128), F32),
            near((2, 256, 128), F32),
            near((WAVES * SLOTS, 128), F32),
            near((WAVES, 3, 8, 128), BF),
            near((WAVES * 8, 128), F32),
            near((WAVES, 3, 8, 128), BF),
            near((NM, NM), BF),
            near((NM, 128), F32),
            near((NM, 256), BF),
            near((RADIX, 72, 2 * SPAN), F32),
            near((80, 128), F32),
            near(message, BF),
            near(message, BF),
            near(halo, BF),
            near(halo, BF),
            near((5, LEVDEV * 24, 128), F32),
            near((5, 4, LEVS, 128), F32),
            near((3, LEVS, 128), F32),
            dma((2,)),
            dma((1,)),
            dma((2,)),
            dma((LEVDEV,)),
            dma((2,)),
            dma((2,)),
        ],
        compiler_params=pltpu.CompilerParams(
            vmem_limit_bytes=60 * 2**20, collective_id=0, has_side_effects=True
        ),
    )(
        wave_numbers,
        wave_numbers.reshape(1, NM),
        spec,
        legendre,
        jnp.asarray(row_table()),
        jnp.asarray(fourier_table()),
        jnp.asarray(edge_table()),
        vertical,
        jnp.asarray(spread_table()),
    )
    return (before - change).reshape(LEVS, 4, 128)


def solution(mesh):
    placed = (P("wave", None, "lev", None), P("wave", None, None), P(), P())
    return jax.shard_map(
        body, mesh=mesh, in_specs=placed, out_specs=P(None, "wave", "lev"), check_vma=False
    )
```
